128 devices in a mesh: dp: 32 (over z, y, core), mp: 4 (over x).
Axes of the slice: x: 4, y: 4, z: 4, core: 2. Of those that a mesh axis runs over, the one named last changes fastest.
Arguments:
- patches: bfloat16 [49152, 128], P(('dp', 'mp')), may hold values from -6 to 6
- row_count: int32 [128], P(('dp', 'mp')), may hold values from 0 to 384, as said below
- target_group: int32 [49152], P(('dp', 'mp')), may hold values from 0 to 31, as said below
- target_offset: int32 [49152], P(('dp', 'mp')), may hold values from 0 to 639, as said below
- embed: bfloat16 [128, 6144], replicated, may hold values from -0.5 to 0.5
- norm_gain: bfloat16 [6144], replicated, may hold values from 0.099609375 to 1.8984375
- readout: bfloat16 [6144, 128], P('mp'), may hold values from -0.078125 to 0.078125
- target: bfloat16 [20480, 128], P('dp'), may hold values from -12 to 12
- master: float32 [6144, 6144], P('dp', 'mp'), may hold values from -6 to 6
- moment1: float32 [6144, 6144], P('dp', 'mp'), may hold values from -2 to 2
- moment2: float32 [6144, 6144], P('dp', 'mp'), may hold values from 0.0034722222 to 0.1388889
Outputs:
- prediction: float32 [20480, 128], P('dp')
- master_new: float32 [6144, 6144], P('dp', 'mp')
- moment1_new: float32 [6144, 6144], P('dp', 'mp')
- moment2_new: float32 [6144, 6144], P('dp', 'mp')
- weight_copy: bfloat16 [6144, 6144], P('dp', 'mp')
The draws below stay inside these ranges and needn't reach their ends.
Inputs may be any that keep to these rules, and one draw needn't show every extreme that they name: Device i holds its live patch rows in its first row_count[i] slots; some device holds 384 of them in every draw. Over the live slots of all devices, each pair (target_group, target_offset) of the 20480 positions occurs exactly once; values in slots past row_count are arbitrary within the range. Call target_offset // 160 the block of a row. Each (batch, block) receives exactly 160 live rows; one device sends at most 3 live rows to one (batch, block), and every (batch, block) gets 3 rows from some device.
All inputs are finite; a program needn't handle non-finite values.
Results may differ from the reference program's by a relative error of at most 0.03.
Values may be sent and summed in bfloat16 or wider, within the bound.
A program may use at most 128 MiB of HBM per device.

```python
import math
import jax
import jax.numpy as jnp
from jax import lax

D = 6144
PATCH = 128
TOK_DEV = 640
TOKENS = 20480
QUART = 160
CAP = 3
SLOTS = 384
N_DP = 32
N_MP = 4
DEVICES = 128


def route_plan(key):
    base_key = jax.random.fold_in(key, 7)
    keys = jax.random.split(base_key, 7)
    devices_all = N_DP * N_MP
    order_draw = jax.random.permutation(keys[0], devices_all)
    heavy_flag = (order_draw < 4).astype(jnp.int32)
    bias_draw = jax.random.randint(keys[1], (devices_all,), 0, 4)
    noise_draw = jax.random.randint(keys[2], (devices_all, devices_all), 0, 65536)
    scores = (heavy_flag * 8 + bias_draw)[None, :] * 65536 + noise_draw
    scores = scores * devices_all + jnp.arange(devices_all, dtype=jnp.int32)[None, :]
    ranking = jnp.argsort(jnp.argsort(-scores, axis=1), axis=1).astype(jnp.int32)
    sent = jnp.clip(QUART - ranking * CAP, 0, CAP).T
    source_rank = ranking.T
    load = jnp.sum(sent, axis=1).astype(jnp.int32)
    cumulative = jnp.cumsum(sent, axis=1)
    starting = cumulative - sent
    slot_ids = jnp.arange(SLOTS, dtype=jnp.int32)
    dest_index = jnp.sum((cumulative[:, None, :] <= slot_ids[None, :, None]).astype(jnp.int32), axis=2)
    dest_clip = jnp.minimum(dest_index, devices_all - 1)
    within = slot_ids[None, :] - jnp.take_along_axis(starting, dest_clip, axis=1)
    rank_here = jnp.take_along_axis(source_rank, dest_clip, axis=1)
    column_perms = jax.vmap(lambda sub_key: jax.random.permutation(sub_key, QUART))(jax.random.split(keys[3], devices_all)).astype(jnp.int32)
    position = jnp.clip(rank_here * CAP + within, 0, QUART - 1)
    local_place = column_perms[dest_clip, position]
    occupied = slot_ids[None, :] < load[:, None]
    group_live = dest_clip // N_MP
    offset_live = dest_clip % N_MP * QUART + local_place
    group_junk = jax.random.randint(keys[4], (devices_all, SLOTS), 0, N_DP)
    offset_junk = jax.random.randint(keys[5], (devices_all, SLOTS), 0, TOK_DEV)
    group_all = jnp.where(occupied, group_live, group_junk).astype(jnp.int32)
    offset_all = jnp.where(occupied, offset_live, offset_junk).astype(jnp.int32)
    shuffle_key = (1 - occupied.astype(jnp.int32)) * 65536 + jax.random.randint(keys[6], (devices_all, SLOTS), 0, 65536)
    shuffle_key = shuffle_key * SLOTS + slot_ids[None, :]
    reorder = jnp.argsort(shuffle_key, axis=1)
    group_all = jnp.take_along_axis(group_all, reorder, axis=1)
    offset_all = jnp.take_along_axis(offset_all, reorder, axis=1)
    return (load, group_all.reshape(-1), offset_all.reshape(-1))


def draw_row_count(key, part):
    return route_plan(key)[0]


def draw_target_group(key, part):
    return route_plan(key)[1]


def draw_target_offset(key, part):
    return route_plan(key)[2]


def shard_levels(stream_key, extent, pieces, low, largest):
    loudness, own = 1.0, jax.random.fold_in(stream_key, 6)
    for dim, shards_of in pieces:
        heights = jnp.exp(jax.random.uniform(jax.random.fold_in(own, dim), (shards_of,), jnp.float32, low / len(pieces), largest / len(pieces)))
        loudness = loudness * jnp.repeat(heights, extent[dim] // shards_of).reshape([-1 if axis == dim else 1 for axis in range(len(extent))])
    return loudness


def centred(stream_key, extent, spread, reach, shards=(), kind=jnp.bfloat16):
    drawn = spread * jax.random.normal(stream_key, extent, jnp.float32)
    if shards:
        drawn = drawn * shard_levels(stream_key, extent, shards, -0.22, 0.18)
    return jnp.clip(drawn, -reach, reach).astype(kind)


def setup_inputs(seed: int = 0) -> dict:
    streams_of = jax.random.split(jax.random.key(seed), 12)
    return {
        "patches": centred(streams_of[0], (DEVICES * SLOTS, PATCH), 1.0, 6.0, ((0, 128),)),
        "row_count": draw_row_count(jax.random.fold_in(streams_of[11], 71), 0),
        "target_group": draw_target_group(jax.random.fold_in(streams_of[11], 71), 0),
        "target_offset": draw_target_offset(jax.random.fold_in(streams_of[11], 71), 0),
        "embed": centred(streams_of[4], (PATCH, D), PATCH ** -0.5, 0.5),
        "norm_gain": jnp.clip(1.0 + 0.18 * jax.random.normal(streams_of[5], (D,), jnp.float32), 0.099609375, 1.8984375).astype(jnp.bfloat16),
        "readout": centred(streams_of[6], (D, PATCH), D ** -0.5, 0.078125, ((0, 4),)),
        "target": centred(streams_of[7], (TOKENS, PATCH), 3.0, 12.0, ((0, 32),)),
        "master": centred(streams_of[8], (D, D), 1.0, 6.0, ((0, 32), (1, 4)), jnp.float32),
        "moment1": centred(streams_of[9], (D, D), 0.3, 2.0, ((0, 32), (1, 4)), jnp.float32),
        "moment2": jnp.clip(jnp.exp(math.log(0.1388889) - 3.6888795 * jax.random.uniform(streams_of[10], (D, D), jnp.float32) ** shard_levels(streams_of[10], (D, D), ((0, 32), (1, 4)), -0.2, 0.2)), 0.0034722222, 0.1388889),
    }


gelu_const = 0.7978845608028654
beta_one = 0.9
beta_two = 0.95
learn_rate = 0.01
decay_rate = 0.1
adam_epsilon = 1e-08
step_count = 20

def gelu_tanh(value):
    inner = gelu_const * (value + 0.044715 * value * value * value)
    return 0.5 * value * (1.0 + jnp.tanh(inner))

def gelu_slope(value):
    tangent = jnp.tanh(gelu_const * (value + 0.044715 * value * value * value))
    return 0.5 * (1.0 + tangent) + 0.5 * value * (1.0 - tangent * tangent) * gelu_const * (1.0 + 3.0 * 0.044715 * value * value)

def reference(patches, row_count, target_group, target_offset, embed, norm_gain, readout, target, master, moment1, moment2):
    occupied = (jnp.arange(SLOTS, dtype=jnp.int32)[None, :] < row_count[:, None]).reshape(-1)
    placed = jnp.where(occupied, target_group * TOK_DEV + target_offset, TOKENS).astype(jnp.int32)
    batch = jnp.zeros((TOKENS, PATCH), jnp.bfloat16).at[placed].set(patches, mode='drop')
    weight = master.astype(jnp.bfloat16)
    width_scale = 1.0 / D ** 0.5
    gain_wide = norm_gain.astype(jnp.float32)

    def group_step(gradient, inputs):
        patch_block, goal = inputs
        hidden = gelu_tanh(jnp.dot(patch_block, embed, preferred_element_type=jnp.float32))
        normed = (hidden * lax.rsqrt(lax.optimization_barrier(jnp.mean(hidden * hidden, axis=-1, keepdims=True)) + 1e-05) * gain_wide).astype(jnp.bfloat16)
        preact = jnp.dot(normed, weight, preferred_element_type=jnp.float32) * width_scale
        activation = gelu_tanh(preact).astype(jnp.bfloat16)
        prediction = jnp.dot(activation, readout, preferred_element_type=jnp.float32)
        errors = (prediction - goal.astype(jnp.float32)).astype(jnp.bfloat16)
        backward = jnp.dot(errors, readout.T, preferred_element_type=jnp.float32)
        delta_rows = (backward * gelu_slope(preact)).astype(jnp.bfloat16)
        term = (jnp.dot(normed.T, delta_rows, preferred_element_type=jnp.float32) * width_scale).astype(jnp.bfloat16)
        term = lax.optimization_barrier(term).astype(jnp.float32)
        return (gradient + term, prediction)
    gradient, predicted = lax.scan(group_step, jnp.zeros((D, D), jnp.float32), (batch.reshape(N_DP, TOK_DEV, PATCH), target.reshape(N_DP, TOK_DEV, PATCH)))
    moment1_new = beta_one * moment1 + (1.0 - beta_one) * gradient
    moment2_new = beta_two * moment2 + (1.0 - beta_two) * gradient * gradient
    first_fix = moment1_new / (1.0 - beta_one ** step_count)
    second_fix = moment2_new / (1.0 - beta_two ** step_count)
    master_new = master - learn_rate * (first_fix / (jnp.sqrt(second_fix) + adam_epsilon) + decay_rate * master)
    return (predicted.reshape(TOKENS, PATCH), master_new, moment1_new, moment2_new, master_new.astype(jnp.bfloat16))
```

```python
import jax
import jax.numpy as jnp
from jax import lax
from jax.experimental import pallas as pl
from jax.experimental.pallas import tpu as pltpu
from jax.sharding import PartitionSpec as P

gelu_const = 0.7978845608028654
cubic = 0.044715
beta_one = 0.9
beta_two = 0.95
learn_rate = 0.01
decay_rate = 0.1
adam_epsilon = 1e-08
step_count = 20

WIDTH = 6144
ROWS = 192
COLS = 768
TOKENS = 1280
BLOCK = 160
SLOTS = 384
SCALE = 1.0 / WIDTH**0.5
MESH = pl.DeviceIdType.MESH
f32, bf16, i32 = jnp.float32, jnp.bfloat16, jnp.int32

NN = (((1,), (0,)), ((), ()))
NT = (((1,), (1,)), ((), ()))
TN = (((0,), (0,)), ((), ()))


def matmul(a, b, dims=NN):
    return lax.dot_general(a, b, dims, preferred_element_type=f32)


def iota(shape, axis):
    return lax.broadcasted_iota(i32, shape, axis)


def kernel(
    row_count,
    patches,
    group_row,
    offset_row,
    gain,
    embed_hbm,
    readout_hbm,
    target_hbm,
    master_hbm,
    pred_out,
    grad_out,
    emb,
    ro,
    tgt,
    master_own,
    master_far,
    far_half,
    w,
    hg,
    acc,
    delta,
    ssq,
    perm,
    out1,
    in1,
    out2,
    in2,
    batch,
    part_out,
    part_in,
    part_own,
    err_own,
    err_in,
    core_in,
    zhalf_in,
    zfull_in,
    y_in,
    pair_in,
    local_sem,
    r1_send,
    r1_recv,
    r2_send,
    r2_recv,
    r3_send,
    r3_recv,
    ag_send,
    ag_recv,
    part_send,
    part_recv,
    err_send,
    err_recv,
    rs_send,
    rs_recv,
):
    dp, x = lax.axis_index("dp"), lax.axis_index("mp")
    z = lax.div(dp, 8)
    y = lax.rem(lax.div(dp, 2), 4)
    c = lax.rem(dp, 2)
    k = lax.div(y, 2)
    p = lax.rem(y, 2)
    half = lax.rem(p + k, 2)
    yp = y + 1 - 2 * p
    ya = 3 - y
    yap = 3 - yp
    kk, oc = 1 - k, 1 - c
    zp, zm, z2 = lax.rem(z + 1, 4), lax.rem(z + 3, 4), lax.rem(z + 2, 4)
    member = z * 4 + k * 2 + c
    sub = p * 4 + x
    zs = (z, zp, zm, z2)
    ys = (y, yp, ya, yap)

    def device(zz, yy, cc, xx):
        return ((zz * 4 + yy) * 2 + cc, xx)

    def member_device(i):
        other = lax.rem(member + i, 16)
        zz, kz, cc = lax.div(other, 4), lax.rem(lax.div(other, 2), 2), lax.rem(other, 2)
        return other, device(zz, 2 * kz + p, cc, x)

    def sub_device(i):
        other = lax.rem(sub + i, 8)
        return other, device(z, 2 * k + lax.div(other, 4), c, lax.rem(other, 4))

    def remote(src, dst, send, recv, to):
        return pltpu.make_async_remote_copy(
            src_ref=src, dst_ref=dst, send_sem=send, recv_sem=recv, device_id=to, device_id_type=MESH
        )

    def chunk(zz, yy, cc, low=0, count=ROWS):
        start = pl.multiple_of(lax.rem(yy, 2) * (2 * ROWS) + cc * ROWS + low, 32)
        return w.at[zz * 2 + lax.div(yy, 2), pl.ds(start, count), :]

    def span(index, size, count=None):
        return pl.ds(pl.multiple_of(index * size, size), size if count is None else count)

    barrier = pltpu.get_barrier_semaphore()
    peers = [member_device(i)[1] for i in range(1, 16)]
    peers += [sub_device(i)[1] for i in range(1, 8)]
    peers += [device(z, ya, c, x)]
    for peer in peers:
        pl.semaphore_signal(barrier, inc=1, device_id=peer, device_id_type=MESH)

    loads = [
        (master_hbm.at[:, span(half, COLS)], master_own),
        (master_hbm.at[:, span(1 - half, COLS)], master_far),
        (embed_hbm, emb),
        (readout_hbm.at[span(half, COLS), :], ro),
        (target_hbm, tgt),
    ]
    loads = [pltpu.make_async_copy(a, b, local_sem.at[i]) for i, (a, b) in enumerate(loads)]
    for load in loads:
        load.start()

    group, offset = group_row[...], offset_row[...]
    live = iota((1, SLOTS), 1) < row_count[0]
    to_member = (group >> 3) * 4 + ((group >> 2) & 1) * 2 + (group & 1)
    block = sum((offset >= BLOCK * i).astype(i32) for i in range(1, 4))
    place = offset - block * BLOCK + 1
    to_sub = ((group >> 1) & 1) * 4 + block
    key = jnp.where(live, to_member * 8 + to_sub, -1)
    row_id, col_id = iota((SLOTS, SLOTS), 0), iota((SLOTS, SLOTS), 1)

    def column(values):
        wide = jnp.broadcast_to(values.astype(f32), (SLOTS, SLOTS))
        return jnp.sum(jnp.where(row_id == col_id, wide, 0.0), axis=1, keepdims=True)

    same = (column(key) == key.astype(f32)) & (row_id < col_id)
    rank = jnp.sum(jnp.where(same, 1.0, 0.0), axis=0, keepdims=True).astype(i32)
    slot = jnp.where(live, to_member * 32 + rank * 8 + to_sub, -1)
    pick = jnp.where(iota((512, SLOTS), 0) == slot, 1.0, 0.0).astype(bf16)
    marks = jnp.broadcast_to(column(place), (SLOTS, 128)).astype(bf16)
    out1[:, :128] = matmul(pick, patches[...]).astype(bf16)
    out1[:, 128:] = matmul(pick, marks).astype(bf16)

    loads[0].wait()
    loads[1].wait()
    own = chunk(z, y, c)
    own[...] = master_own[...].astype(bf16)
    far_half[...] = master_far[...].astype(bf16)

    pl.semaphore_wait(barrier, len(peers))

    sends = []

    def launch(copy):
        copy.start()
        sends.append(copy)

    for i in range(1, 16):
        other, to = member_device(i)
        launch(
            remote(
                out1.at[span(other, 32), :],
                in1.at[span(member, 32), :],
                r1_send.at[other],
                r1_recv.at[member],
                to,
            )
        )

    gathers = []

    def gather(event, src, dst, to):
        copy = remote(src, dst, ag_send.at[event], ag_recv.at[event], to)
        copy.start()
        gathers.append(copy)

    def gathered(event, dst):
        remote(dst, dst, ag_send.at[event], ag_recv.at[event], device(z, y, oc, x)).wait_recv()

    def along_z(event, zz, yy, low=0, count=ROWS, up=True):
        piece = chunk(zz, yy, c, low, count)
        gather(event, piece, piece, device(zp if up else zm, y, c, x))

    def full_z(event, yy):
        along_z(event, z, yy)
        along_z(event + 1, z, yy, up=False)

    def halves_z(event, yy):
        along_z(event + 2, zm, yy, 0, ROWS // 2)
        along_z(event + 3, zp, yy, ROWS // 2, ROWS // 2, up=False)

    def wait_full(event, yy):
        gathered(event, chunk(zm, yy, c))
        gathered(event + 1, chunk(zp, yy, c))

    def wait_halves(event, yy):
        gathered(event + 2, chunk(z2, yy, c, 0, ROWS // 2))
        gathered(event + 3, chunk(z2, yy, c, ROWS // 2, ROWS // 2))

    def along_y(j):
        piece = chunk(zs[j], yp, c)
        gather(14 + j, piece, piece, device(z, ya, c, x))

    def wait_y(j):
        gathered(14 + j, chunk(zs[j], yap, c))

    def relay(j, l):
        piece = chunk(zs[j], ys[l], c)
        gather(18 + j * 4 + l, piece, piece, device(z, y, oc, x))

    def wait_relay(j, l):
        gathered(18 + j * 4 + l, chunk(zs[j], ys[l], oc))

    gather(0, far_half, own, device(z, yp, c, x))
    gather(1, own, own, device(z, ya, c, x))
    full_z(2, y)
    relay(0, 0)

    in1[span(member, 32), :] = out1[span(member, 32), :]
    row512 = iota((512, 512), 0)
    source = (row512 & 15) * 32 + ((row512 >> 4) & 3) * 8 + (row512 >> 6)
    perm[...] = jnp.where(iota((512, 512), 1) == source, 1.0, 0.0).astype(bf16)
    for i in range(1, 16):
        other, to = member_device(i)
        landed = in1.at[span(other, 32), :]
        remote(landed, landed, r1_send.at[other], r1_recv.at[other], to).wait_recv()
    out2[...] = matmul(perm[...], in1[...]).astype(bf16)
    for i in range(1, 8):
        other, to = sub_device(i)
        launch(
            remote(
                out2.at[span(other, 64, 48), :],
                in2.at[span(sub, 48), :],
                r2_send.at[other],
                r2_recv.at[sub],
                to,
            )
        )
    in2[span(sub, 48), :] = out2[span(sub, 64, 48), :]

    gathered(0, chunk(z, yp, c))
    full_z(10, yp)
    along_y(0)
    relay(0, 1)

    for i in range(1, 8):
        other, to = sub_device(i)
        landed = in2.at[span(other, 48), :]
        remote(landed, landed, r2_send.at[other], r2_recv.at[other], to).wait_recv()
    mark = in2[:, 128:].astype(f32)
    lane = iota((SLOTS, 128), 1)
    to_place = jnp.concatenate(
        [
            jnp.where(mark == (lane + 1).astype(f32), 1.0, 0.0),
            jnp.where(mark == (lane + 129).astype(f32), 1.0, 0.0),
        ],
        axis=1,
    ).astype(bf16)
    mine = span(sub, BLOCK)
    batch[mine, :] = matmul(to_place, in2[:, :128], TN)[:BLOCK].astype(bf16)
    for i in range(1, 8):
        other, to = sub_device(i)
        launch(remote(batch.at[mine, :], batch.at[mine, :], r3_send.at[other], r3_recv.at[sub], to))

    wait_full(2, y)
    relay(1, 0)
    relay(2, 0)
    gathered(1, chunk(z, ya, c))
    relay(0, 2)

    for i in range(1, 8):
        other, to = sub_device(i)
        landed = batch.at[span(other, BLOCK), :]
        remote(landed, landed, r3_send.at[other], r3_recv.at[other], to).wait_recv()
    loads[2].wait()

    def embed(j):
        def tile(i, carry):
            rows = span(i, 128)
            v = matmul(batch[rows, :], emb[:, j * COLS : (j + 1) * COLS])
            t = jnp.tanh(v * (gelu_const + (gelu_const * cubic) * (v * v)))
            twice = v + v * t
            square = twice * twice
            total = sum(square[:, l * 128 : (l + 1) * 128] for l in range(COLS // 128))
            ssq[rows, :] = total if j == 0 else ssq[rows, :] + total
            hg[j, rows, :] = (twice * gain[j]).astype(bf16)
            return carry

        lax.fori_loop(0, TOKENS // 128, tile, 0)

    def forward(zz, kx, first=False):
        g = zz * 2 + kx

        def tile(i, carry):
            rows = span(i, 256)
            term = matmul(hg[g, rows, :], w[g])
            acc[rows, :] = term if first else acc[rows, :] + term
            return carry

        lax.fori_loop(0, TOKENS // 256, tile, 0)

    embed(0)
    embed(1)
    wait_full(10, yp)
    halves_z(10, yp)
    along_y(1)
    along_y(2)
    full_z(6, ya)
    relay(1, 1)
    relay(2, 1)
    embed(2)
    embed(3)
    wait_halves(10, yp)
    along_y(3)
    halves_z(2, y)
    relay(3, 1)
    wait_y(0)
    relay(0, 3)
    for j in range(4, 8):
        embed(j)
    for l in range(2):
        wait_relay(0, l)
    forward(z, k, first=True)
    wait_full(6, ya)
    halves_z(6, ya)
    relay(1, 2)
    relay(2, 2)
    for j in (1, 2):
        for l in range(2):
            wait_relay(j, l)
        forward(zs[j], k)
    wait_halves(2, y)
    relay(3, 0)
    for l in range(2, 4):
        wait_relay(0, l)
    forward(z, kk)
    wait_y(1)
    relay(1, 3)
    wait_y(2)
    relay(2, 3)
    for l in range(2):
        wait_relay(3, l)
    forward(z2, k)
    wait_halves(6, ya)
    relay(3, 2)
    for j in (1, 2):
        for l in range(2, 4):
            wait_relay(j, l)
        forward(zs[j], kk)
    wait_y(3)
    relay(3, 3)
    for l in range(2, 4):
        wait_relay(3, l)
    forward(z2, kk)

    loads[3].wait()
    loads[4].wait()

    def row_scale(rows):
        mean4 = jnp.sum(ssq[rows, :], axis=1, keepdims=True) * (0.25 / WIDTH)
        return lax.rsqrt(mean4 + 1e-05) * (0.5 * SCALE)

    def partial(index):
        rows = span(index, BLOCK)
        v = acc[rows, :] * row_scale(rows)
        t = jnp.tanh(v * (gelu_const + (gelu_const * cubic) * (v * v)))
        return matmul((0.5 * v * (1.0 + t)).astype(bf16), ro[...])

    for i in range(1, 8):
        other, to = sub_device(i)
        part_out[other] = partial(other).astype(bf16)
        launch(
            remote(part_out.at[other], part_in.at[sub], part_send.at[other], part_recv.at[sub], to)
        )
    part_own[...] = partial(sub)

    def slope(i, carry):
        rows = span(i, BLOCK)
        r = row_scale(rows)
        v = acc[rows, :] * r
        t = jnp.tanh(v * (gelu_const + (gelu_const * cubic) * (v * v)))
        acc[rows, :] = r * (
            0.5 * (1.0 + t)
            + (0.5 * gelu_const) * v * (1.0 - t * t) * (1.0 + (3.0 * cubic) * (v * v))
        )
        return carry

    lax.fori_loop(0, 8, slope, 0)
    total = part_own[...]
    for i in range(1, 8):
        other, to = sub_device(i)
        landed = part_in.at[other]
        remote(landed, landed, part_send.at[other], part_recv.at[other], to).wait_recv()
        total = total + part_in[other].astype(f32)
    total = total.astype(bf16)
    err_in[sub] = total
    err_own[...] = (total.astype(f32) - tgt[span(x, BLOCK), :].astype(f32)).astype(bf16)
    for i in range(4):
        other = lax.rem(x + i, 4)
        launch(
            remote(
                err_own,
                err_in.at[sub],
                err_send.at[(1 - p) * 4 + other],
                err_recv.at[sub],
                device(z, yp, c, other),
            )
        )
        if i:
            launch(
                remote(
                    err_in.at[sub],
                    err_in.at[sub],
                    err_send.at[p * 4 + other],
                    err_recv.at[sub],
                    device(z, y, c, other),
                )
            )

    def backward(index, errors):
        rows = span(index, BLOCK)
        delta[rows, :] = (matmul(errors, ro[...], NT) * acc[rows, :]).astype(bf16)

    for i in range(4):
        other = lax.rem(x + i, 4)
        index = p * 4 + other
        landed = err_in.at[index]
        if i:
            to = device(z, y, c, other)
            remote(landed, landed, err_send.at[index], err_recv.at[index], to).wait_recv()
        rows = span(other, BLOCK)
        pred_out[rows, :] = err_in[index]
        backward(index, (err_in[index].astype(f32) - tgt[rows, :].astype(f32)).astype(bf16))
    for i in range(4):
        other = lax.rem(x + i, 4)
        index = (1 - p) * 4 + other
        landed = err_in.at[index]
        to = device(z, yp, c, other)
        remote(landed, landed, err_send.at[index], err_recv.at[index], to).wait_recv()
        backward(index, err_in[index])

    for copy in gathers:
        copy.wait_send()

    def scatter(event, src, dst, to):
        launch(remote(src, dst, rs_send.at[event], rs_recv.at[event], to))

    def scattered(event, dst):
        remote(dst, dst, rs_send.at[event], rs_recv.at[event], device(z, y, oc, x)).wait_recv()

    def add(target, terms, count=ROWS):
        def tile(i, carry):
            rows = span(i, 48)
            value = target[rows, :].astype(f32)
            for term in terms:
                value = value + term[rows, :].astype(f32)
            target[rows, :] = value.astype(bf16)
            return carry

        lax.fori_loop(0, count // 48, tile, 0)

    def core_slot(zz, yy):
        start = pl.multiple_of(lax.rem(yy, 2) * ROWS, 32)
        return core_in.at[zz * 2 + lax.div(yy, 2), pl.ds(start, ROWS), :]

    def gradient(j, far):
        zz = zs[j]
        g = zz * 2 + (kk if far else k)

        def tile(i, carry):
            rows = span(i, 256)
            w[g, rows, :] = matmul(hg[g, :, rows], delta[...], TN).astype(bf16)
            return carry

        lax.fori_loop(0, 3, tile, 0)
        for l in (3, 2) if far else (0, 1):
            scatter(j * 4 + l, chunk(zz, ys[l], oc), core_slot(zz, ys[l]), device(z, y, oc, x))

    def cores(j, l):
        scattered(j * 4 + l, core_slot(zs[j], ys[l]))
        add(chunk(zs[j], ys[l], c), [core_slot(zs[j], ys[l])])

    kinds = {0: y, 1: ya, 2: yp}
    down, up = device(zm, y, c, x), device(zp, y, c, x)

    def send_halves(kind):
        yy = kinds[kind]
        event = 16 + 4 * kind
        scatter(event, chunk(z2, yy, c, 0, ROWS // 2), zhalf_in.at[kind, 0], down)
        scatter(event + 1, chunk(z2, yy, c, ROWS // 2, ROWS // 2), zhalf_in.at[kind, 1], up)

    def send_full(kind, side):
        yy = kinds[kind]
        event = 16 + 4 * kind + side
        zz = (zm, zp)[side]
        scattered(event, zhalf_in.at[kind, side])
        add(
            chunk(zz, yy, c, side * (ROWS // 2), ROWS // 2),
            [zhalf_in.at[kind, side]],
            ROWS // 2,
        )
        scatter(event + 2, chunk(zz, yy, c), zfull_in.at[kind, side], (down, up)[side])

    def wait_fulls(kind):
        for side in range(2):
            scattered(18 + 4 * kind + side, zfull_in.at[kind, side])
        return [zfull_in.at[kind, side] for side in range(2)]

    def send_y(j):
        scatter(28 + j, chunk(zs[j], yap, c), y_in.at[j], device(z, ya, c, x))

    def take_y(j):
        scattered(28 + j, y_in.at[j])
        add(chunk(zs[j], yp, c), [y_in.at[j]])

    gradient(3, True)
    gradient(3, False)
    cores(3, 3)
    send_y(3)
    cores(3, 2)
    send_halves(1)
    gradient(1, True)
    cores(3, 0)
    send_halves(0)
    gradient(2, True)
    cores(1, 3)
    send_y(1)
    gradient(1, False)
    cores(2, 3)
    send_y(2)
    cores(1, 2)
    send_full(1, 1)
    cores(2, 2)
    send_full(1, 0)
    gradient(2, False)
    cores(3, 1)
    take_y(3)
    send_halves(2)
    cores(1, 0)
    send_full(0, 1)
    gradient(0, True)
    cores(2, 0)
    send_full(0, 0)
    gradient(0, False)
    cores(0, 3)
    send_y(0)
    cores(1, 1)
    cores(2, 1)
    take_y(1)
    send_full(2, 1)
    take_y(2)
    send_full(2, 0)
    cores(0, 2)
    add(chunk(z, ya, c), wait_fulls(1))
    scatter(32, chunk(z, ya, c), y_in.at[4], device(z, ya, c, x))
    cores(0, 1)
    cores(0, 0)
    take_y(0)
    add(chunk(z, yp, c), wait_fulls(2))
    scatter(33, chunk(z, yp, c), pair_in, device(z, yp, c, x))
    terms = wait_fulls(0)
    scattered(32, y_in.at[4])
    terms = terms + [y_in.at[4]]

    def finish(i, carry):
        rows = span(i, 48)
        value = own[rows, :].astype(f32)
        for term in terms:
            value = value + term[rows, :].astype(f32)
        grad_out[rows, span(half, COLS)] = value
        return carry

    lax.fori_loop(0, ROWS // 48, finish, 0)
    scattered(33, pair_in)
    grad_out[:, span(1 - half, COLS)] = pair_in[...].astype(f32)
    for copy in sends:
        copy.wait_send()


def step(row_count, patches, group, offset, gain, embed, readout, target, master):
    vmem = pl.BlockSpec(memory_space=pltpu.VMEM)
    smem = pl.BlockSpec(memory_space=pltpu.SMEM)
    hbm = pl.BlockSpec(memory_space=pl.ANY)
    dma = pltpu.SemaphoreType.DMA
    return pl.pallas_call(
        kernel,
        out_shape=(
            jax.ShapeDtypeStruct((640, 128), bf16),
            jax.ShapeDtypeStruct((ROWS, 2 * COLS), f32),
        ),
        in_specs=[smem, vmem, vmem, vmem, vmem, hbm, hbm, hbm, hbm],
        out_specs=(vmem, vmem),
        scratch_shapes=[
            pltpu.VMEM((128, WIDTH), bf16),
            pltpu.VMEM((COLS, 128), bf16),
            pltpu.VMEM((640, 128), bf16),
            pltpu.VMEM((ROWS, COLS), f32),
            pltpu.VMEM((ROWS, COLS), f32),
            pltpu.VMEM((ROWS, COLS), bf16),
            pltpu.VMEM((8, COLS, COLS), bf16),
            pltpu.VMEM((8, TOKENS, COLS), bf16),
            pltpu.VMEM((TOKENS, COLS), f32),
            pltpu.VMEM((TOKENS, COLS), bf16),
            pltpu.VMEM((TOKENS, 128), f32),
            pltpu.VMEM((512, 512), bf16),
            pltpu.VMEM((512, 256), bf16),
            pltpu.VMEM((512, 256), bf16),
            pltpu.VMEM((512, 256), bf16),
            pltpu.VMEM((SLOTS, 256), bf16),
            pltpu.VMEM((TOKENS, 128), bf16),
            pltpu.VMEM((8, BLOCK, 128), bf16),
            pltpu.VMEM((8, BLOCK, 128), bf16),
            pltpu.VMEM((BLOCK, 128), f32),
            pltpu.VMEM((BLOCK, 128), bf16),
            pltpu.VMEM((8, BLOCK, 128), bf16),
            pltpu.VMEM((8, 2 * ROWS, COLS), bf16),
            pltpu.VMEM((3, 2, ROWS // 2, COLS), bf16),
            pltpu.VMEM((3, 2, ROWS, COLS), bf16),
            pltpu.VMEM((5, ROWS, COLS), bf16),
            pltpu.VMEM((ROWS, COLS), bf16),
            dma((5,)),
            dma((16,)),
            dma((16,)),
            dma((8,)),
            dma((8,)),
            dma((8,)),
            dma((8,)),
            dma((34,)),
            dma((34,)),
            dma((8,)),
            dma((8,)),
            dma((8,)),
            dma((8,)),
            dma((34,)),
            dma((34,)),
        ],
        compiler_params=pltpu.CompilerParams(
            collective_id=0, has_side_effects=True, vmem_limit_bytes=56 * 1024 * 1024
        ),
        name="train_step",
    )(row_count, patches, group, offset, gain, embed, readout, target, master)


def shards(
    patches,
    row_count,
    target_group,
    target_offset,
    embed,
    norm_gain,
    readout,
    target,
    master,
    moment1,
    moment2,
):
    prediction, gradient = step(
        row_count,
        patches,
        target_group.reshape(1, SLOTS),
        target_offset.reshape(1, SLOTS),
        norm_gain.astype(f32).reshape(8, 1, COLS),
        embed,
        readout,
        target,
        master,
    )
    moment1_new = beta_one * moment1 + (1.0 - beta_one) * gradient
    moment2_new = beta_two * moment2 + (1.0 - beta_two) * gradient * gradient
    first_fix = moment1_new / (1.0 - beta_one**step_count)
    second_fix = moment2_new / (1.0 - beta_two**step_count)
    master_new = master - learn_rate * (
        first_fix / (jnp.sqrt(second_fix) + adam_epsilon) + decay_rate * master
    )
    return (
        prediction.astype(f32),
        master_new,
        moment1_new,
        moment2_new,
        master_new.astype(bf16),
    )


def solution(mesh):
    placed = (
        P(("dp", "mp"), None),
        P(("dp", "mp")),
        P(("dp", "mp")),
        P(("dp", "mp")),
        P(),
        P(),
        P("mp", None),
        P("dp", None),
        P("dp", "mp"),
        P("dp", "mp"),
        P("dp", "mp"),
    )
    return jax.shard_map(
        shards,
        mesh=mesh,
        in_specs=placed,
        out_specs=(P("dp", None), P("dp", "mp"), P("dp", "mp"), P("dp", "mp"), P("dp", "mp")),
        check_vma=False,
    )
```

```python
import jax
import jax.numpy as jnp
from jax import lax
from jax.experimental import pallas as pl
from jax.experimental.pallas import tpu as pltpu
from jax.sharding import PartitionSpec as P

gelu_const = 0.7978845608028654
cubic = 0.044715
beta_one = 0.9
beta_two = 0.95
learn_rate = 0.01
decay_rate = 0.1
adam_epsilon = 1e-08
step_count = 20

WIDTH = 6144
ROWS = 192
COLS = 768
TOKENS = 1280
BLOCK = 160
SLOTS = 384
SCALE = 1.0 / WIDTH**0.5
MESH = pl.DeviceIdType.MESH
f32, bf16, i32 = jnp.float32, jnp.bfloat16, jnp.int32

NN = (((1,), (0,)), ((), ()))
NT = (((1,), (1,)), ((), ()))
TN = (((0,), (0,)), ((), ()))


def matmul(a, b, dims=NN):
    return lax.dot_general(a, b, dims, preferred_element_type=f32)


def iota(shape, axis):
    return lax.broadcasted_iota(i32, shape, axis)


def kernel(
    row_count,
    patches,
    group_row,
    offset_row,
    gain,
    embed_hbm,
    readout_hbm,
    target_hbm,
    master_hbm,
    pred_out,
    grad_out,
    emb,
    ro,
    tgt,
    master_own,
    master_far,
    far_half,
    w,
    hg,
    acc,
    delta,
    ssq,
    perm,
    out1,
    in1,
    out2,
    in2,
    batch,
    part_out,
    part_in,
    part_own,
    err_own,
    err_in,
    core_in,
    zhalf_in,
    zfull_in,
    y_in,
    pair_in,
    local_sem,
    r1_send,
    r1_recv,
    r2_send,
    r2_recv,
    r3_send,
    r3_recv,
    ag_send,
    ag_recv,
    part_send,
    part_recv,
    err_send,
    err_recv,
    rs_send,
    rs_recv,
):
    dp, x = lax.axis_index("dp"), lax.axis_index("mp")
    z = lax.div(dp, 8)
    y = lax.rem(lax.div(dp, 2), 4)
    c = lax.rem(dp, 2)
    k = lax.div(y, 2)
    p = lax.rem(y, 2)
    half = lax.rem(p + k, 2)
    yp = y + 1 - 2 * p
    ya = 3 - y
    yap = 3 - yp
    kk, oc = 1 - k, 1 - c
    zp, zm, z2 = lax.rem(z + 1, 4), lax.rem(z + 3, 4), lax.rem(z + 2, 4)
    member = z * 4 + k * 2 + c
    sub = p * 4 + x
    zs = (z, zp, zm, z2)
    ys = (y, yp, ya, yap)

    def device(zz, yy, cc, xx):
        return ((zz * 4 + yy) * 2 + cc, xx)

    def member_device(i):
        other = lax.rem(member + i, 16)
        zz, kz, cc = lax.div(other, 4), lax.rem(lax.div(other, 2), 2), lax.rem(other, 2)
        return other, device(zz, 2 * kz + p, cc, x)

    def sub_device(i):
        other = lax.rem(sub + i, 8)
        return other, device(z, 2 * k + lax.div(other, 4), c, lax.rem(other, 4))

    def remote(src, dst, send, recv, to):
        return pltpu.make_async_remote_copy(
            src_ref=src, dst_ref=dst, send_sem=send, recv_sem=recv, device_id=to, device_id_type=MESH
        )

    def chunk(zz, yy, cc, low=0, count=ROWS):
        start = pl.multiple_of(lax.rem(yy, 2) * (2 * ROWS) + cc * ROWS + low, 32)
        return w.at[zz * 2 + lax.div(yy, 2), pl.ds(start, count), :]

    def span(index, size, count=None):
        return pl.ds(pl.multiple_of(index * size, size), size if count is None else count)

    barrier = pltpu.get_barrier_semaphore()
    peers = [member_device(i)[1] for i in range(1, 16)]
    peers += [sub_device(i)[1] for i in range(1, 8)]
    peers += [device(z, ya, c, x)]
    for peer in peers:
        pl.semaphore_signal(barrier, inc=1, device_id=peer, device_id_type=MESH)

    loads = [
        (master_hbm.at[:, span(half, COLS)], master_own),
        (master_hbm.at[:, span(1 - half, COLS)], master_far),
        (embed_hbm, emb),
        (readout_hbm.at[span(half, COLS), :], ro),
        (target_hbm, tgt),
    ]
    loads = [pltpu.make_async_copy(a, b, local_sem.at[i]) for i, (a, b) in enumerate(loads)]
    for load in loads:
        load.start()

    def as_row(ref):
        return jnp.concatenate([ref[i : i + 1, :] for i in range(SLOTS // 128)], axis=1)

    group, offset = as_row(group_row), as_row(offset_row)
    live = iota((1, SLOTS), 1) < row_count[0]
    to_member = (group >> 3) * 4 + ((group >> 2) & 1) * 2 + (group & 1)
    block = sum((offset >= BLOCK * i).astype(i32) for i in range(1, 4))
    place = offset - block * BLOCK + 1
    to_sub = ((group >> 1) & 1) * 4 + block
    key = jnp.where(live, to_member * 8 + to_sub, -1)
    row_id, col_id = iota((SLOTS, SLOTS), 0), iota((SLOTS, SLOTS), 1)

    def column(values):
        wide = jnp.broadcast_to(values.astype(f32), (SLOTS, SLOTS))
        return jnp.sum(jnp.where(row_id == col_id, wide, 0.0), axis=1, keepdims=True)

    same = (column(key) == key.astype(f32)) & (row_id < col_id)
    rank = jnp.sum(jnp.where(same, 1.0, 0.0), axis=0, keepdims=True).astype(i32)
    slot = jnp.where(live, to_member * 32 + rank * 8 + to_sub, -1)
    pick = jnp.where(iota((512, SLOTS), 0) == slot, 1.0, 0.0).astype(bf16)
    marks = jnp.broadcast_to(column(place), (SLOTS, 128)).astype(bf16)
    out1[:, :128] = matmul(pick, patches[...]).astype(bf16)
    out1[:, 128:] = matmul(pick, marks).astype(bf16)

    loads[0].wait()
    loads[1].wait()
    own = chunk(z, y, c)
    own[...] = master_own[...].astype(bf16)
    far_half[...] = master_far[...].astype(bf16)

    pl.semaphore_wait(barrier, len(peers))

    sends = []

    def launch(copy):
        copy.start()
        sends.append(copy)

    for i in range(1, 16):
        other, to = member_device(i)
        launch(
            remote(
                out1.at[span(other, 32), :],
                in1.at[span(member, 32), :],
                r1_send.at[other],
                r1_recv.at[member],
                to,
            )
        )

    gathers = []

    def gather(event, src, dst, to):
        copy = remote(src, dst, ag_send.at[event], ag_recv.at[event], to)
        copy.start()
        gathers.append(copy)

    def gathered(event, dst):
        remote(dst, dst, ag_send.at[event], ag_recv.at[event], device(z, y, oc, x)).wait_recv()

    def along_z(event, zz, yy, low=0, count=ROWS, up=True):
        piece = chunk(zz, yy, c, low, count)
        gather(event, piece, piece, device(zp if up else zm, y, c, x))

    def full_z(event, yy):
        along_z(event, z, yy)
        along_z(event + 1, z, yy, up=False)

    def halves_z(event, yy):
        along_z(event + 2, zm, yy, 0, ROWS // 2)
        along_z(event + 3, zp, yy, ROWS // 2, ROWS // 2, up=False)

    def wait_full(event, yy):
        gathered(event, chunk(zm, yy, c))
        gathered(event + 1, chunk(zp, yy, c))

    def wait_halves(event, yy):
        gathered(event + 2, chunk(z2, yy, c, 0, ROWS // 2))
        gathered(event + 3, chunk(z2, yy, c, ROWS // 2, ROWS // 2))

    def along_y(j):
        piece = chunk(zs[j], yp, c)
        gather(14 + j, piece, piece, device(z, ya, c, x))

    def wait_y(j):
        gathered(14 + j, chunk(zs[j], yap, c))

    def relay(j, l):
        piece = chunk(zs[j], ys[l], c)
        gather(18 + j * 4 + l, piece, piece, device(z, y, oc, x))

    def wait_relay(j, l):
        gathered(18 + j * 4 + l, chunk(zs[j], ys[l], oc))

    gather(0, far_half, own, device(z, yp, c, x))
    gather(1, own, own, device(z, ya, c, x))
    full_z(2, y)
    relay(0, 0)

    in1[span(member, 32), :] = out1[span(member, 32), :]
    row512 = iota((512, 512), 0)
    source = (row512 & 15) * 32 + ((row512 >> 4) & 3) * 8 + (row512 >> 6)
    perm[...] = jnp.where(iota((512, 512), 1) == source, 1.0, 0.0).astype(bf16)
    for i in range(1, 16):
        other, to = member_device(i)
        landed = in1.at[span(other, 32), :]
        remote(landed, landed, r1_send.at[other], r1_recv.at[other], to).wait_recv()
    out2[...] = matmul(perm[...], in1[...]).astype(bf16)
    for i in range(1, 8):
        other, to = sub_device(i)
        launch(
            remote(
                out2.at[span(other, 64, 48), :],
                in2.at[span(sub, 48), :],
                r2_send.at[other],
                r2_recv.at[sub],
                to,
            )
        )
    in2[span(sub, 48), :] = out2[span(sub, 64, 48), :]

    gathered(0, chunk(z, yp, c))
    full_z(10, yp)
    along_y(0)
    relay(0, 1)

    for i in range(1, 8):
        other, to = sub_device(i)
        landed = in2.at[span(other, 48), :]
        remote(landed, landed, r2_send.at[other], r2_recv.at[other], to).wait_recv()
    mark = in2[:, 128:].astype(f32)
    lane = iota((SLOTS, 128), 1)
    to_place = jnp.concatenate(
        [
            jnp.where(mark == (lane + 1).astype(f32), 1.0, 0.0),
            jnp.where(mark == (lane + 129).astype(f32), 1.0, 0.0),
        ],
        axis=1,
    ).astype(bf16)
    mine = span(sub, BLOCK)
    batch[mine, :] = matmul(to_place, in2[:, :128], TN)[:BLOCK].astype(bf16)
    for i in range(1, 8):
        other, to = sub_device(i)
        launch(remote(batch.at[mine, :], batch.at[mine, :], r3_send.at[other], r3_recv.at[sub], to))

    wait_full(2, y)
    relay(1, 0)
    relay(2, 0)
    gathered(1, chunk(z, ya, c))
    relay(0, 2)
    wait_full(10, yp)
    along_y(1)
    along_y(2)
    halves_z(10, yp)
    full_z(6, ya)
    relay(1, 1)
    relay(2, 1)

    for i in range(1, 8):
        other, to = sub_device(i)
        landed = batch.at[span(other, BLOCK), :]
        remote(landed, landed, r3_send.at[other], r3_recv.at[other], to).wait_recv()
    loads[2].wait()

    def embed(j):
        v = matmul(batch[...], emb[:, j * COLS : (j + 1) * COLS])
        t = jnp.tanh(v * (gelu_const + (gelu_const * cubic) * (v * v)))
        twice = v + v * t
        square = twice * twice
        total = sum(square[:, l * 128 : (l + 1) * 128] for l in range(COLS // 128))
        ssq[...] = total if j == 0 else ssq[...] + total
        gains = gain[...].astype(f32)
        lanes = COLS // 128
        gain_row = jnp.concatenate([gains[lanes * j + l : lanes * j + l + 1] for l in range(lanes)], axis=1)
        hg[j] = (twice * gain_row).astype(bf16)

    def forward(zz, kx, first=False):
        g = zz * 2 + kx
        term = matmul(hg[g], w[g])
        acc[...] = term if first else acc[...] + term

    embed(0)
    embed(1)
    embed(2)
    wait_halves(10, yp)
    along_y(3)
    halves_z(2, y)
    relay(3, 1)
    wait_y(0)
    relay(0, 3)
    embed(3)
    embed(4)
    embed(5)
    wait_full(6, ya)
    halves_z(6, ya)
    relay(1, 2)
    relay(2, 2)
    embed(6)
    embed(7)
    for l in range(2):
        wait_relay(0, l)
    forward(z, k, first=True)
    for j in (1, 2):
        for l in range(2):
            wait_relay(j, l)
        forward(zs[j], k)
    wait_y(1)
    relay(1, 3)
    wait_y(2)
    relay(2, 3)
    wait_halves(2, y)
    relay(3, 0)
    for l in range(2, 4):
        wait_relay(0, l)
    forward(z, kk)
    wait_halves(6, ya)
    relay(3, 2)
    for l in range(2):
        wait_relay(3, l)
    forward(z2, k)
    for j in (1, 2):
        for l in range(2, 4):
            wait_relay(j, l)
        forward(zs[j], kk)
    wait_y(3)
    relay(3, 3)
    for l in range(2, 4):
        wait_relay(3, l)
    forward(z2, kk)

    loads[3].wait()
    loads[4].wait()

    def row_scale(rows):
        mean4 = jnp.sum(ssq[rows, :], axis=1, keepdims=True) * (0.25 / WIDTH)
        return lax.rsqrt(mean4 + 1e-05) * (0.5 * SCALE)

    def partial(index):
        rows = span(index, BLOCK)
        v = acc[rows, :] * row_scale(rows)
        t = jnp.tanh(v * (gelu_const + (gelu_const * cubic) * (v * v)))
        return matmul((0.5 * v * (1.0 + t)).astype(bf16), ro[...])

    for i in range(1, 8):
        other, to = sub_device(i)
        part_out[other] = partial(other).astype(bf16)
        launch(
            remote(part_out.at[other], part_in.at[sub], part_send.at[other], part_recv.at[sub], to)
        )
    part_own[...] = partial(sub)

    def slope(i, carry):
        rows = span(i, BLOCK)
        r = row_scale(rows)
        v = acc[rows, :] * r
        t = jnp.tanh(v * (gelu_const + (gelu_const * cubic) * (v * v)))
        acc[rows, :] = r * (
            0.5 * (1.0 + t)
            + (0.5 * gelu_const) * v * (1.0 - t * t) * (1.0 + (3.0 * cubic) * (v * v))
        )
        return carry

    lax.fori_loop(0, 8, slope, 0)
    total = part_own[...]
    for i in range(1, 8):
        other, to = sub_device(i)
        landed = part_in.at[other]
        remote(landed, landed, part_send.at[other], part_recv.at[other], to).wait_recv()
        total = total + part_in[other].astype(f32)
    total = total.astype(bf16)
    err_in[sub] = total
    err_own[...] = (total.astype(f32) - tgt[span(x, BLOCK), :].astype(f32)).astype(bf16)
    for i in range(4):
        other = lax.rem(x + i, 4)
        launch(
            remote(
                err_own,
                err_in.at[sub],
                err_send.at[(1 - p) * 4 + other],
                err_recv.at[sub],
                device(z, yp, c, other),
            )
        )
        if i:
            launch(
                remote(
                    err_in.at[sub],
                    err_in.at[sub],
                    err_send.at[p * 4 + other],
                    err_recv.at[sub],
                    device(z, y, c, other),
                )
            )

    def backward(index, errors):
        rows = span(index, BLOCK)
        delta[rows, :] = (matmul(errors, ro[...], NT) * acc[rows, :]).astype(bf16)

    for i in range(4):
        other = lax.rem(x + i, 4)
        index = p * 4 + other
        landed = err_in.at[index]
        if i:
            to = device(z, y, c, other)
            remote(landed, landed, err_send.at[index], err_recv.at[index], to).wait_recv()
        rows = span(other, BLOCK)
        pred_out[rows, :] = err_in[index]
        backward(index, (err_in[index].astype(f32) - tgt[rows, :].astype(f32)).astype(bf16))
    for i in range(4):
        other = lax.rem(x + i, 4)
        index = (1 - p) * 4 + other
        landed = err_in.at[index]
        to = device(z, yp, c, other)
        remote(landed, landed, err_send.at[index], err_recv.at[index], to).wait_recv()
        backward(index, err_in[index])

    for copy in gathers:
        copy.wait_send()

    def scatter(event, src, dst, to):
        launch(remote(src, dst, rs_send.at[event], rs_recv.at[event], to))

    def scattered(event, dst):
        remote(dst, dst, rs_send.at[event], rs_recv.at[event], device(z, y, oc, x)).wait_recv()

    def add(target, terms, count=ROWS):
        def tile(i, carry):
            rows = span(i, 48)
            value = target[rows, :].astype(f32)
            for term in terms:
                value = value + term[rows, :].astype(f32)
            target[rows, :] = value.astype(bf16)
            return carry

        lax.fori_loop(0, count // 48, tile, 0)

    def core_slot(zz, yy):
        start = pl.multiple_of(lax.rem(yy, 2) * ROWS, 32)
        return core_in.at[zz * 2 + lax.div(yy, 2), pl.ds(start, ROWS), :]

    def gradient(j, far):
        zz = zs[j]
        g = zz * 2 + (kk if far else k)

        w[g] = matmul(hg[g], delta[...], TN).astype(bf16)
        for l in (3, 2) if far else (0, 1):
            scatter(j * 4 + l, chunk(zz, ys[l], oc), core_slot(zz, ys[l]), device(z, y, oc, x))

    def cores(j, l):
        scattered(j * 4 + l, core_slot(zs[j], ys[l]))
        add(chunk(zs[j], ys[l], c), [core_slot(zs[j], ys[l])])

    kinds = {0: y, 1: ya, 2: yp}
    down, up = device(zm, y, c, x), device(zp, y, c, x)

    def send_halves(kind):
        yy = kinds[kind]
        event = 16 + 4 * kind
        scatter(event, chunk(z2, yy, c, 0, ROWS // 2), zhalf_in.at[kind, 0], down)
        scatter(event + 1, chunk(z2, yy, c, ROWS // 2, ROWS // 2), zhalf_in.at[kind, 1], up)

    def send_full(kind, side):
        yy = kinds[kind]
        event = 16 + 4 * kind + side
        zz = (zm, zp)[side]
        scattered(event, zhalf_in.at[kind, side])
        add(
            chunk(zz, yy, c, side * (ROWS // 2), ROWS // 2),
            [zhalf_in.at[kind, side]],
            ROWS // 2,
        )
        scatter(event + 2, chunk(zz, yy, c), zfull_in.at[kind, side], (down, up)[side])

    def wait_fulls(kind):
        for side in range(2):
            scattered(18 + 4 * kind + side, zfull_in.at[kind, side])
        return [zfull_in.at[kind, side] for side in range(2)]

    def send_y(j):
        scatter(28 + j, chunk(zs[j], yap, c), y_in.at[j], device(z, ya, c, x))

    def take_y(j):
        scattered(28 + j, y_in.at[j])
        add(chunk(zs[j], yp, c), [y_in.at[j]])

    gradient(3, True)
    cores(3, 3)
    send_y(3)
    cores(3, 2)
    send_halves(1)
    gradient(3, False)
    gradient(1, True)
    cores(3, 0)
    send_halves(0)
    cores(3, 1)
    gradient(2, True)
    gradient(1, False)
    cores(1, 3)
    cores(2, 3)
    take_y(3)
    send_halves(2)
    send_y(1)
    send_y(2)
    cores(1, 2)
    send_full(1, 1)
    cores(2, 2)
    send_full(1, 0)
    gradient(2, False)
    cores(1, 0)
    send_full(0, 1)
    gradient(0, True)
    cores(2, 0)
    send_full(0, 0)
    gradient(0, False)
    cores(1, 1)
    cores(2, 1)
    for l in (3, 2, 1, 0):
        cores(0, l)
    take_y(1)
    send_full(2, 1)
    take_y(2)
    send_y(0)
    send_full(2, 0)
    add(chunk(z, ya, c), wait_fulls(1))
    take_y(0)
    scatter(32, chunk(z, ya, c), y_in.at[4], device(z, ya, c, x))
    add(chunk(z, yp, c), wait_fulls(2))
    scatter(33, chunk(z, yp, c), pair_in, device(z, yp, c, x))
    terms = wait_fulls(0)
    scattered(32, y_in.at[4])
    terms = terms + [y_in.at[4]]

    def finish(i, carry):
        rows = span(i, 48)
        value = own[rows, :].astype(f32)
        for term in terms:
            value = value + term[rows, :].astype(f32)
        grad_out[rows, span(half, COLS)] = value
        return carry

    lax.fori_loop(0, ROWS // 48, finish, 0)
    scattered(33, pair_in)
    grad_out[:, span(1 - half, COLS)] = pair_in[...].astype(f32)
    for copy in sends:
        copy.wait_send()


def step(row_count, patches, group, offset, gain, embed, readout, target, master):
    vmem = pl.BlockSpec(memory_space=pltpu.VMEM)
    smem = pl.BlockSpec(memory_space=pltpu.SMEM)
    hbm = pl.BlockSpec(memory_space=pl.ANY)
    dma = pltpu.SemaphoreType.DMA
    return pl.pallas_call(
        kernel,
        out_shape=(
            jax.ShapeDtypeStruct((640, 128), bf16),
            jax.ShapeDtypeStruct((ROWS, 2 * COLS), f32),
        ),
        in_specs=[smem, vmem, vmem, vmem, vmem, hbm, hbm, hbm, hbm],
        out_specs=(vmem, vmem),
        scratch_shapes=[
            pltpu.VMEM((128, WIDTH), bf16),
            pltpu.VMEM((COLS, 128), bf16),
            pltpu.VMEM((640, 128), bf16),
            pltpu.VMEM((ROWS, COLS), f32),
            pltpu.VMEM((ROWS, COLS), f32),
            pltpu.VMEM((ROWS, COLS), bf16),
            pltpu.VMEM((8, COLS, COLS), bf16),
            pltpu.VMEM((8, TOKENS, COLS), bf16),
            pltpu.VMEM((TOKENS, COLS), f32),
            pltpu.VMEM((TOKENS, COLS), bf16),
            pltpu.VMEM((TOKENS, 128), f32),
            pltpu.VMEM((512, 512), bf16),
            pltpu.VMEM((512, 256), bf16),
            pltpu.VMEM((512, 256), bf16),
            pltpu.VMEM((512, 256), bf16),
            pltpu.VMEM((SLOTS, 256), bf16),
            pltpu.VMEM((TOKENS, 128), bf16),
            pltpu.VMEM((8, BLOCK, 128), bf16),
            pltpu.VMEM((8, BLOCK, 128), bf16),
            pltpu.VMEM((BLOCK, 128), f32),
            pltpu.VMEM((BLOCK, 128), bf16),
            pltpu.VMEM((8, BLOCK, 128), bf16),
            pltpu.VMEM((8, 2 * ROWS, COLS), bf16),
            pltpu.VMEM((3, 2, ROWS // 2, COLS), bf16),
            pltpu.VMEM((3, 2, ROWS, COLS), bf16),
            pltpu.VMEM((5, ROWS, COLS), bf16),
            pltpu.VMEM((ROWS, COLS), bf16),
            dma((5,)),
            dma((16,)),
            dma((16,)),
            dma((8,)),
            dma((8,)),
            dma((8,)),
            dma((8,)),
            dma((34,)),
            dma((34,)),
            dma((8,)),
            dma((8,)),
            dma((8,)),
            dma((8,)),
            dma((34,)),
            dma((34,)),
        ],
        compiler_params=pltpu.CompilerParams(
            collective_id=0, has_side_effects=True, vmem_limit_bytes=56 * 1024 * 1024
        ),
        name="train_step",
    )(row_count, patches, group, offset, gain, embed, readout, target, master)


def shards(
    patches,
    row_count,
    target_group,
    target_offset,
    embed,
    norm_gain,
    readout,
    target,
    master,
    moment1,
    moment2,
):
    prediction, gradient = step(
        row_count,
        patches,
        target_group.reshape(3, 128),
        target_offset.reshape(3, 128),
        norm_gain.reshape(48, 128),
        embed,
        readout,
        target,
        master,
    )
    moment1_new = beta_one * moment1 + (1.0 - beta_one) * gradient
    moment2_new = beta_two * moment2 + (1.0 - beta_two) * gradient * gradient
    first_fix = moment1_new / (1.0 - beta_one**step_count)
    second_fix = moment2_new / (1.0 - beta_two**step_count)
    master_new = master - learn_rate * (
        first_fix / (jnp.sqrt(second_fix) + adam_epsilon) + decay_rate * master
    )
    return (
        prediction.astype(f32),
        master_new,
        moment1_new,
        moment2_new,
        master_new.astype(bf16),
    )


def solution(mesh):
    placed = (
        P(("dp", "mp"), None),
        P(("dp", "mp")),
        P(("dp", "mp")),
        P(("dp", "mp")),
        P(),
        P(),
        P("mp", None),
        P("dp", None),
        P("dp", "mp"),
        P("dp", "mp"),
        P("dp", "mp"),
    )
    return jax.shard_map(
        shards,
        mesh=mesh,
        in_specs=placed,
        out_specs=(P("dp", None), P("dp", "mp"), P("dp", "mp"), P("dp", "mp"), P("dp", "mp")),
        check_vma=False,
    )
```

```python
import jax
import jax.numpy as jnp
from jax import lax
from jax.experimental import pallas as pl
from jax.experimental.pallas import tpu as pltpu
from jax.sharding import PartitionSpec as P

gelu_const = 0.7978845608028654
cubic = 0.044715
beta_one = 0.9
beta_two = 0.95
learn_rate = 0.01
decay_rate = 0.1
adam_epsilon = 1e-08
step_count = 20

WIDTH = 6144
ROWS = 192
COLS = 768
TOKENS = 1280
BLOCK = 160
SLOTS = 384
SCALE = 1.0 / WIDTH**0.5
MESH = pl.DeviceIdType.MESH
f32, bf16, i32 = jnp.float32, jnp.bfloat16, jnp.int32

NN = (((1,), (0,)), ((), ()))
NT = (((1,), (1,)), ((), ()))
TN = (((0,), (0,)), ((), ()))


def matmul(a, b, dims=NN):
    return lax.dot_general(a, b, dims, preferred_element_type=f32)


def iota(shape, axis):
    return lax.broadcasted_iota(i32, shape, axis)


def kernel(
    row_count,
    patches,
    group_row,
    offset_row,
    gain,
    embed_hbm,
    readout_hbm,
    target_hbm,
    master_hbm,
    pred_out,
    grad_out,
    emb,
    ro,
    tgt,
    master_own,
    master_far,
    far_half,
    w,
    hg,
    acc,
    delta,
    ssq,
    perm,
    out1,
    in1,
    out2,
    in2,
    batch,
    part_out,
    part_in,
    part_own,
    err_own,
    err_in,
    core_in,
    zhalf_in,
    zfull_in,
    y_in,
    pair_in,
    local_sem,
    r1_send,
    r1_recv,
    r2_send,
    r2_recv,
    r3_send,
    r3_recv,
    ag_send,
    ag_recv,
    part_send,
    part_recv,
    err_send,
    err_recv,
    rs_send,
    rs_recv,
):
    dp, x = lax.axis_index("dp"), lax.axis_index("mp")
    z = lax.div(dp, 8)
    y = lax.rem(lax.div(dp, 2), 4)
    c = lax.rem(dp, 2)
    k = lax.div(y, 2)
    p = lax.rem(y, 2)
    half = lax.rem(p + k, 2)
    yp = y + 1 - 2 * p
    ya = 3 - y
    yap = 3 - yp
    kk, oc = 1 - k, 1 - c
    zp, zm, z2 = lax.rem(z + 1, 4), lax.rem(z + 3, 4), lax.rem(z + 2, 4)
    member = z * 4 + k * 2 + c
    sub = p * 4 + x
    zs = (z, zp, zm, z2)
    ys = (y, yp, ya, yap)

    def device(zz, yy, cc, xx):
        return ((zz * 4 + yy) * 2 + cc, xx)

    def member_device(i):
        other = lax.rem(member + i, 16)
        zz, kz, cc = lax.div(other, 4), lax.rem(lax.div(other, 2), 2), lax.rem(other, 2)
        return other, device(zz, 2 * kz + p, cc, x)

    def sub_device(i):
        other = lax.rem(sub + i, 8)
        return other, device(z, 2 * k + lax.div(other, 4), c, lax.rem(other, 4))

    def remote(src, dst, send, recv, to):
        return pltpu.make_async_remote_copy(
            src_ref=src, dst_ref=dst, send_sem=send, recv_sem=recv, device_id=to, device_id_type=MESH
        )

    def chunk(zz, yy, cc, low=0, count=ROWS):
        start = pl.multiple_of(lax.rem(yy, 2) * (2 * ROWS) + cc * ROWS + low, 32)
        return w.at[zz * 2 + lax.div(yy, 2), pl.ds(start, count), :]

    def span(index, size, count=None):
        return pl.ds(pl.multiple_of(index * size, size), size if count is None else count)

    barrier = pltpu.get_barrier_semaphore()
    peers = [member_device(i)[1] for i in range(1, 16)]
    peers += [sub_device(i)[1] for i in range(1, 8)]
    peers += [device(z, ya, c, x)]
    for peer in peers:
        pl.semaphore_signal(barrier, inc=1, device_id=peer, device_id_type=MESH)

    loads = [
        (master_hbm.at[:, span(half, COLS)], master_own),
        (master_hbm.at[:, span(1 - half, COLS)], master_far),
        (embed_hbm, emb),
        (readout_hbm.at[span(half, COLS), :], ro),
        (target_hbm, tgt),
    ]
    loads = [pltpu.make_async_copy(a, b, local_sem.at[i]) for i, (a, b) in enumerate(loads)]
    for load in loads:
        load.start()

    def as_row(ref):
        return jnp.concatenate([ref[i : i + 1, :] for i in range(SLOTS // 128)], axis=1)

    group, offset = as_row(group_row), as_row(offset_row)
    live = iota((1, SLOTS), 1) < row_count[0]
    to_member = (group >> 3) * 4 + ((group >> 2) & 1) * 2 + (group & 1)
    block = sum((offset >= BLOCK * i).astype(i32) for i in range(1, 4))
    place = offset - block * BLOCK + 1
    to_sub = ((group >> 1) & 1) * 4 + block
    key = jnp.where(live, to_member * 8 + to_sub, -1)
    row_id, col_id = iota((SLOTS, SLOTS), 0), iota((SLOTS, SLOTS), 1)

    def column(values):
        wide = jnp.broadcast_to(values.astype(f32), (SLOTS, SLOTS))
        return jnp.sum(jnp.where(row_id == col_id, wide, 0.0), axis=1, keepdims=True)

    same = (column(key) == key.astype(f32)) & (row_id < col_id)
    rank = jnp.sum(jnp.where(same, 1.0, 0.0), axis=0, keepdims=True).astype(i32)
    slot = jnp.where(live, to_member * 32 + rank * 8 + to_sub, -1)
    pick = jnp.where(iota((512, SLOTS), 0) == slot, 1.0, 0.0).astype(bf16)
    marks = jnp.broadcast_to(column(place), (SLOTS, 128)).astype(bf16)
    out1[:, :128] = matmul(pick, patches[...]).astype(bf16)
    out1[:, 128:] = matmul(pick, marks).astype(bf16)

    loads[0].wait()
    loads[1].wait()
    own = chunk(z, y, c)
    own[...] = master_own[...].astype(bf16)
    far_half[...] = master_far[...].astype(bf16)

    pl.semaphore_wait(barrier, len(peers))

    sends = []

    def launch(copy):
        copy.start()
        sends.append(copy)

    for i in range(1, 16):
        other, to = member_device(i)
        launch(
            remote(
                out1.at[span(other, 32), :],
                in1.at[span(member, 32), :],
                r1_send.at[other],
                r1_recv.at[member],
                to,
            )
        )

    gathers = []

    def gather(event, src, dst, to):
        copy = remote(src, dst, ag_send.at[event], ag_recv.at[event], to)
        copy.start()
        gathers.append(copy)

    def gathered(event, dst):
        remote(dst, dst, ag_send.at[event], ag_recv.at[event], device(z, y, oc, x)).wait_recv()

    def along_z(event, zz, yy, low=0, count=ROWS, up=True):
        piece = chunk(zz, yy, c, low, count)
        gather(event, piece, piece, device(zp if up else zm, y, c, x))

    def full_z(event, yy):
        along_z(event, z, yy)
        along_z(event + 1, z, yy, up=False)

    def halves_z(event, yy):
        along_z(event + 2, zm, yy, 0, ROWS // 2)
        along_z(event + 3, zp, yy, ROWS // 2, ROWS // 2, up=False)

    def wait_full(event, yy):
        gathered(event, chunk(zm, yy, c))
        gathered(event + 1, chunk(zp, yy, c))

    def wait_halves(event, yy):
        gathered(event + 2, chunk(z2, yy, c, 0, ROWS // 2))
        gathered(event + 3, chunk(z2, yy, c, ROWS // 2, ROWS // 2))

    def along_y(j):
        piece = chunk(zs[j], yp, c)
        gather(14 + j, piece, piece, device(z, ya, c, x))

    def wait_y(j):
        gathered(14 + j, chunk(zs[j], yap, c))

    def relay(j, l):
        piece = chunk(zs[j], ys[l], c)
        gather(18 + j * 4 + l, piece, piece, device(z, y, oc, x))

    def wait_relay(j, l):
        gathered(18 + j * 4 + l, chunk(zs[j], ys[l], oc))

    gather(0, far_half, own, device(z, yp, c, x))
    gather(1, own, own, device(z, ya, c, x))
    full_z(2, y)
    relay(0, 0)

    in1[span(member, 32), :] = out1[span(member, 32), :]
    row512 = iota((512, 512), 0)
    source = (row512 & 15) * 32 + ((row512 >> 4) & 3) * 8 + (row512 >> 6)
    perm[...] = jnp.where(iota((512, 512), 1) == source, 1.0, 0.0).astype(bf16)
    for i in range(1, 16):
        other, to = member_device(i)
        landed = in1.at[span(other, 32), :]
        remote(landed, landed, r1_send.at[other], r1_recv.at[other], to).wait_recv()
    out2[...] = matmul(perm[...], in1[...]).astype(bf16)
    for i in range(1, 8):
        other, to = sub_device(i)
        launch(
            remote(
                out2.at[span(other, 64, 48), :],
                in2.at[span(sub, 48), :],
                r2_send.at[other],
                r2_recv.at[sub],
                to,
            )
        )
    in2[span(sub, 48), :] = out2[span(sub, 64, 48), :]

    gathered(0, chunk(z, yp, c))
    full_z(10, yp)
    along_y(0)
    relay(0, 1)

    for i in range(1, 8):
        other, to = sub_device(i)
        landed = in2.at[span(other, 48), :]
        remote(landed, landed, r2_send.at[other], r2_recv.at[other], to).wait_recv()
    mark = in2[:, 128:].astype(f32)
    lane = iota((SLOTS, 128), 1)
    to_place = jnp.concatenate(
        [
            jnp.where(mark == (lane + 1).astype(f32), 1.0, 0.0),
            jnp.where(mark == (lane + 129).astype(f32), 1.0, 0.0),
        ],
        axis=1,
    ).astype(bf16)
    mine = span(sub, BLOCK)
    batch[mine, :] = matmul(to_place, in2[:, :128], TN)[:BLOCK].astype(bf16)
    for i in range(1, 8):
        other, to = sub_device(i)
        launch(remote(batch.at[mine, :], batch.at[mine, :], r3_send.at[other], r3_recv.at[sub], to))

    wait_full(2, y)
    relay(1, 0)
    relay(2, 0)
    gathered(1, chunk(z, ya, c))
    relay(0, 2)
    wait_full(10, yp)
    along_y(1)
    along_y(2)
    halves_z(10, yp)
    full_z(6, ya)
    relay(1, 1)
    relay(2, 1)

    for i in range(1, 8):
        other, to = sub_device(i)
        landed = batch.at[span(other, BLOCK), :]
        remote(landed, landed, r3_send.at[other], r3_recv.at[other], to).wait_recv()
    loads[2].wait()

    def embed(j):
        v = matmul(batch[...], emb[:, j * COLS : (j + 1) * COLS])
        t = jnp.tanh(v * (gelu_const + (gelu_const * cubic) * (v * v)))
        twice = v + v * t
        square = twice * twice
        total = sum(square[:, l * 128 : (l + 1) * 128] for l in range(COLS // 128))
        ssq[...] = total if j == 0 else ssq[...] + total
        gains = gain[...].astype(f32)
        lanes = COLS // 128
        gain_row = jnp.concatenate([gains[lanes * j + l : lanes * j + l + 1] for l in range(lanes)], axis=1)
        hg[j] = (twice * gain_row).astype(bf16)

    def forward(zz, kx, first=False):
        g = zz * 2 + kx
        term = matmul(hg[g], w[g])
        acc[...] = term if first else acc[...] + term

    embed(0)
    embed(1)
    embed(2)
    wait_halves(10, yp)
    along_y(3)
    halves_z(2, y)
    relay(3, 1)
    wait_y(0)
    relay(0, 3)
    embed(3)
    embed(4)
    embed(5)
    wait_full(6, ya)
    halves_z(6, ya)
    relay(1, 2)
    relay(2, 2)
    embed(6)
    embed(7)
    for l in range(2):
        wait_relay(0, l)
    forward(z, k, first=True)
    for l in range(2, 4):
        wait_relay(0, l)
    forward(z, kk)
    for j in (1, 2):
        for l in range(2):
            wait_relay(j, l)
        forward(zs[j], k)
    wait_halves(2, y)
    relay(3, 0)
    wait_halves(6, ya)
    relay(3, 2)
    for l in range(2):
        wait_relay(3, l)
    forward(z2, k)
    wait_y(1)
    relay(1, 3)
    wait_y(2)
    relay(2, 3)
    for j in (1, 2):
        for l in range(2, 4):
            wait_relay(j, l)
        forward(zs[j], kk)
    wait_y(3)
    relay(3, 3)
    for l in range(2, 4):
        wait_relay(3, l)
    forward(z2, kk)

    loads[3].wait()
    loads[4].wait()

    def row_scale(rows):
        mean4 = jnp.sum(ssq[rows, :], axis=1, keepdims=True) * (0.25 / WIDTH)
        return lax.rsqrt(mean4 + 1e-05) * (0.5 * SCALE)

    def partial(index):
        rows = span(index, BLOCK)
        v = acc[rows, :] * row_scale(rows)
        t = jnp.tanh(v * (gelu_const + (gelu_const * cubic) * (v * v)))
        return matmul((0.5 * v * (1.0 + t)).astype(bf16), ro[...])

    for i in range(1, 8):
        other, to = sub_device(i)
        part_out[other] = partial(other).astype(bf16)
        launch(
            remote(part_out.at[other], part_in.at[sub], part_send.at[other], part_recv.at[sub], to)
        )
    part_own[...] = partial(sub)

    def slope(i, carry):
        rows = span(i, BLOCK)
        r = row_scale(rows)
        v = acc[rows, :] * r
        t = jnp.tanh(v * (gelu_const + (gelu_const * cubic) * (v * v)))
        acc[rows, :] = r * (
            0.5 * (1.0 + t)
            + (0.5 * gelu_const) * v * (1.0 - t * t) * (1.0 + (3.0 * cubic) * (v * v))
        )
        return carry

    lax.fori_loop(0, 8, slope, 0)
    total = part_own[...]
    for i in range(1, 8):
        other, to = sub_device(i)
        landed = part_in.at[other]
        remote(landed, landed, part_send.at[other], part_recv.at[other], to).wait_recv()
        total = total + part_in[other].astype(f32)
    total = total.astype(bf16)
    err_in[sub] = total
    err_own[...] = (total.astype(f32) - tgt[span(x, BLOCK), :].astype(f32)).astype(bf16)
    for i in range(4):
        other = lax.rem(x + i, 4)
        launch(
            remote(
                err_own,
                err_in.at[sub],
                err_send.at[(1 - p) * 4 + other],
                err_recv.at[sub],
                device(z, yp, c, other),
            )
        )
        if i:
            launch(
                remote(
                    err_in.at[sub],
                    err_in.at[sub],
                    err_send.at[p * 4 + other],
                    err_recv.at[sub],
                    device(z, y, c, other),
                )
            )

    def backward(index, errors):
        rows = span(index, BLOCK)
        delta[rows, :] = (matmul(errors, ro[...], NT) * acc[rows, :]).astype(bf16)

    for i in range(4):
        other = lax.rem(x + i, 4)
        index = p * 4 + other
        landed = err_in.at[index]
        if i:
            to = device(z, y, c, other)
            remote(landed, landed, err_send.at[index], err_recv.at[index], to).wait_recv()
        rows = span(other, BLOCK)
        pred_out[rows, :] = err_in[index]
        backward(index, (err_in[index].astype(f32) - tgt[rows, :].astype(f32)).astype(bf16))
    for i in range(4):
        other = lax.rem(x + i, 4)
        index = (1 - p) * 4 + other
        landed = err_in.at[index]
        to = device(z, yp, c, other)
        remote(landed, landed, err_send.at[index], err_recv.at[index], to).wait_recv()
        backward(index, err_in[index])

    for copy in gathers:
        copy.wait_send()

    def scatter(event, src, dst, to):
        launch(remote(src, dst, rs_send.at[event], rs_recv.at[event], to))

    def scattered(event, dst):
        remote(dst, dst, rs_send.at[event], rs_recv.at[event], device(z, y, oc, x)).wait_recv()

    def add(target, terms, count=ROWS):
        def tile(i, carry):
            rows = span(i, 48)
            value = target[rows, :].astype(f32)
            for term in terms:
                value = value + term[rows, :].astype(f32)
            target[rows, :] = value.astype(bf16)
            return carry

        lax.fori_loop(0, count // 48, tile, 0)

    def core_slot(zz, yy):
        start = pl.multiple_of(lax.rem(yy, 2) * ROWS, 32)
        return core_in.at[zz * 2 + lax.div(yy, 2), pl.ds(start, ROWS), :]

    def gradient(j, far):
        zz = zs[j]
        g = zz * 2 + (kk if far else k)


        def tile(i, carry):
            rows = span(i, 384)
            w[g, rows, :] = matmul(hg[g, :, rows], delta[...], TN).astype(bf16)
            return carry

        lax.fori_loop(0, 2, tile, 0)
        for l in (3, 2) if far else (0, 1):
            scatter(j * 4 + l, chunk(zz, ys[l], oc), core_slot(zz, ys[l]), device(z, y, oc, x))

    def cores(j, l):
        scattered(j * 4 + l, core_slot(zs[j], ys[l]))
        add(chunk(zs[j], ys[l], c), [core_slot(zs[j], ys[l])])

    kinds = {0: y, 1: ya, 2: yp}
    down, up = device(zm, y, c, x), device(zp, y, c, x)

    def send_halves(kind):
        yy = kinds[kind]
        event = 16 + 4 * kind
        scatter(event, chunk(z2, yy, c, 0, ROWS // 2), zhalf_in.at[kind, 0], down)
        scatter(event + 1, chunk(z2, yy, c, ROWS // 2, ROWS // 2), zhalf_in.at[kind, 1], up)

    def send_full(kind, side):
        yy = kinds[kind]
        event = 16 + 4 * kind + side
        zz = (zm, zp)[side]
        scattered(event, zhalf_in.at[kind, side])
        add(
            chunk(zz, yy, c, side * (ROWS // 2), ROWS // 2),
            [zhalf_in.at[kind, side]],
            ROWS // 2,
        )
        scatter(event + 2, chunk(zz, yy, c), zfull_in.at[kind, side], (down, up)[side])

    def wait_fulls(kind):
        for side in range(2):
            scattered(18 + 4 * kind + side, zfull_in.at[kind, side])
        return [zfull_in.at[kind, side] for side in range(2)]

    def send_y(j):
        scatter(28 + j, chunk(zs[j], yap, c), y_in.at[j], device(z, ya, c, x))

    def take_y(j):
        scattered(28 + j, y_in.at[j])
        add(chunk(zs[j], yp, c), [y_in.at[j]])

    gradient(3, True)
    cores(3, 3)
    send_y(3)
    cores(3, 2)
    send_halves(1)
    gradient(3, False)
    cores(3, 0)
    send_halves(0)
    gradient(1, True)
    cores(1, 3)
    send_y(1)
    cores(3, 1)
    gradient(2, True)
    cores(2, 3)
    send_y(2)
    take_y(3)
    send_halves(2)
    cores(1, 2)
    send_full(1, 1)
    cores(2, 2)
    send_full(1, 0)
    gradient(1, False)
    cores(1, 0)
    send_full(0, 1)
    gradient(2, False)
    cores(2, 0)
    send_full(0, 0)
    gradient(0, True)
    cores(0, 3)
    send_y(0)
    gradient(0, False)
    cores(1, 1)
    cores(2, 1)
    cores(0, 2)
    take_y(1)
    send_full(2, 1)
    take_y(2)
    send_full(2, 0)
    add(chunk(z, ya, c), wait_fulls(1))
    scatter(32, chunk(z, ya, c), y_in.at[4], device(z, ya, c, x))
    cores(0, 1)
    cores(0, 0)
    take_y(0)
    add(chunk(z, yp, c), wait_fulls(2))
    scatter(33, chunk(z, yp, c), pair_in, device(z, yp, c, x))
    terms = wait_fulls(0)
    scattered(32, y_in.at[4])
    terms = terms + [y_in.at[4]]

    def finish(i, carry):
        rows = span(i, 48)
        value = own[rows, :].astype(f32)
        for term in terms:
            value = value + term[rows, :].astype(f32)
        grad_out[rows, span(half, COLS)] = value
        return carry

    lax.fori_loop(0, ROWS // 48, finish, 0)
    scattered(33, pair_in)
    grad_out[:, span(1 - half, COLS)] = pair_in[...].astype(f32)
    for copy in sends:
        copy.wait_send()


def step(row_count, patches, group, offset, gain, embed, readout, target, master):
    vmem = pl.BlockSpec(memory_space=pltpu.VMEM)
    smem = pl.BlockSpec(memory_space=pltpu.SMEM)
    hbm = pl.BlockSpec(memory_space=pl.ANY)
    dma = pltpu.SemaphoreType.DMA
    return pl.pallas_call(
        kernel,
        out_shape=(
            jax.ShapeDtypeStruct((640, 128), bf16),
            jax.ShapeDtypeStruct((ROWS, 2 * COLS), f32),
        ),
        in_specs=[smem, vmem, vmem, vmem, vmem, hbm, hbm, hbm, hbm],
        out_specs=(vmem, vmem),
        scratch_shapes=[
            pltpu.VMEM((128, WIDTH), bf16),
            pltpu.VMEM((COLS, 128), bf16),
            pltpu.VMEM((640, 128), bf16),
            pltpu.VMEM((ROWS, COLS), f32),
            pltpu.VMEM((ROWS, COLS), f32),
            pltpu.VMEM((ROWS, COLS), bf16),
            pltpu.VMEM((8, COLS, COLS), bf16),
            pltpu.VMEM((8, TOKENS, COLS), bf16),
            pltpu.VMEM((TOKENS, COLS), f32),
            pltpu.VMEM((TOKENS, COLS), bf16),
            pltpu.VMEM((TOKENS, 128), f32),
            pltpu.VMEM((512, 512), bf16),
            pltpu.VMEM((512, 256), bf16),
            pltpu.VMEM((512, 256), bf16),
            pltpu.VMEM((512, 256), bf16),
            pltpu.VMEM((SLOTS, 256), bf16),
            pltpu.VMEM((TOKENS, 128), bf16),
            pltpu.VMEM((8, BLOCK, 128), bf16),
            pltpu.VMEM((8, BLOCK, 128), bf16),
            pltpu.VMEM((BLOCK, 128), f32),
            pltpu.VMEM((BLOCK, 128), bf16),
            pltpu.VMEM((8, BLOCK, 128), bf16),
            pltpu.VMEM((8, 2 * ROWS, COLS), bf16),
            pltpu.VMEM((3, 2, ROWS // 2, COLS), bf16),
            pltpu.VMEM((3, 2, ROWS, COLS), bf16),
            pltpu.VMEM((5, ROWS, COLS), bf16),
            pltpu.VMEM((ROWS, COLS), bf16),
            dma((5,)),
            dma((16,)),
            dma((16,)),
            dma((8,)),
            dma((8,)),
            dma((8,)),
            dma((8,)),
            dma((34,)),
            dma((34,)),
            dma((8,)),
            dma((8,)),
            dma((8,)),
            dma((8,)),
            dma((34,)),
            dma((34,)),
        ],
        compiler_params=pltpu.CompilerParams(
            collective_id=0, has_side_effects=True, vmem_limit_bytes=56 * 1024 * 1024
        ),
        name="train_step",
    )(row_count, patches, group, offset, gain, embed, readout, target, master)


def shards(
    patches,
    row_count,
    target_group,
    target_offset,
    embed,
    norm_gain,
    readout,
    target,
    master,
    moment1,
    moment2,
):
    prediction, gradient = step(
        row_count,
        patches,
        target_group.reshape(3, 128),
        target_offset.reshape(3, 128),
        norm_gain.reshape(48, 128),
        embed,
        readout,
        target,
        master,
    )
    moment1_new = beta_one * moment1 + (1.0 - beta_one) * gradient
    moment2_new = beta_two * moment2 + (1.0 - beta_two) * gradient * gradient
    first_fix = moment1_new / (1.0 - beta_one**step_count)
    second_fix = moment2_new / (1.0 - beta_two**step_count)
    master_new = master - learn_rate * (
        first_fix / (jnp.sqrt(second_fix) + adam_epsilon) + decay_rate * master
    )
    return (
        prediction.astype(f32),
        master_new,
        moment1_new,
        moment2_new,
        master_new.astype(bf16),
    )


def solution(mesh):
    placed = (
        P(("dp", "mp"), None),
        P(("dp", "mp")),
        P(("dp", "mp")),
        P(("dp", "mp")),
        P(),
        P(),
        P("mp", None),
        P("dp", None),
        P("dp", "mp"),
        P("dp", "mp"),
        P("dp", "mp"),
    )
    return jax.shard_map(
        shards,
        mesh=mesh,
        in_specs=placed,
        out_specs=(P("dp", None), P("dp", "mp"), P("dp", "mp"), P("dp", "mp"), P("dp", "mp")),
        check_vma=False,
    )
```

```python
import jax
import jax.numpy as jnp
from jax import lax
from jax.experimental import pallas as pl
from jax.experimental.pallas import tpu as pltpu
from jax.sharding import PartitionSpec as P

gelu_const = 0.7978845608028654
cubic = 0.044715
beta_one = 0.9
beta_two = 0.95
learn_rate = 0.01
decay_rate = 0.1
adam_epsilon = 1e-08
step_count = 20

WIDTH = 6144
ROWS = 192
COLS = 768
TOKENS = 1280
BLOCK = 160
SLOTS = 384
SCALE = 1.0 / WIDTH**0.5
MESH = pl.DeviceIdType.MESH
f32, bf16, i32 = jnp.float32, jnp.bfloat16, jnp.int32

NN = (((1,), (0,)), ((), ()))
NT = (((1,), (1,)), ((), ()))
TN = (((0,), (0,)), ((), ()))


def matmul(a, b, dims=NN):
    return lax.dot_general(a, b, dims, preferred_element_type=f32)


def iota(shape, axis):
    return lax.broadcasted_iota(i32, shape, axis)


def kernel(
    row_count,
    patches,
    group_row,
    offset_row,
    gain,
    embed_hbm,
    readout_hbm,
    target_hbm,
    master_hbm,
    pred_out,
    grad_out,
    emb,
    ro,
    tgt,
    master_own,
    master_far,
    far_half,
    w,
    hg,
    acc,
    delta,
    ssq,
    gain_rows,
    perm,
    out1,
    in1,
    out2,
    in2,
    batch,
    part_out,
    part_in,
    part_own,
    err_own,
    err_in,
    core_in,
    zhalf_in,
    zfull_in,
    y_in,
    pair_in,
    local_sem,
    r1_send,
    r1_recv,
    r2_send,
    r2_recv,
    r3_send,
    r3_recv,
    ag_send,
    ag_recv,
    part_send,
    part_recv,
    err_send,
    err_recv,
    rs_send,
    rs_recv,
):
    dp, x = lax.axis_index("dp"), lax.axis_index("mp")
    z = lax.div(dp, 8)
    y = lax.rem(lax.div(dp, 2), 4)
    c = lax.rem(dp, 2)
    k = lax.div(y, 2)
    p = lax.rem(y, 2)
    half = lax.rem(p + k, 2)
    yp = y + 1 - 2 * p
    ya = 3 - y
    yap = 3 - yp
    kk, oc = 1 - k, 1 - c
    zp, zm, z2 = lax.rem(z + 1, 4), lax.rem(z + 3, 4), lax.rem(z + 2, 4)
    member = z * 4 + k * 2 + c
    sub = p * 4 + x
    zs = (z, zp, zm, z2)
    ys = (y, yp, ya, yap)

    def device(zz, yy, cc, xx):
        return ((zz * 4 + yy) * 2 + cc, xx)

    def member_device(i):
        other = lax.rem(member + i, 16)
        zz, kz, cc = lax.div(other, 4), lax.rem(lax.div(other, 2), 2), lax.rem(other, 2)
        return other, device(zz, 2 * kz + p, cc, x)

    def sub_device(i):
        other = lax.rem(sub + i, 8)
        return other, device(z, 2 * k + lax.div(other, 4), c, lax.rem(other, 4))

    def remote(src, dst, send, recv, to):
        return pltpu.make_async_remote_copy(
            src_ref=src, dst_ref=dst, send_sem=send, recv_sem=recv, device_id=to, device_id_type=MESH
        )

    def chunk(zz, yy, cc, low=0, count=ROWS):
        start = pl.multiple_of(lax.rem(yy, 2) * (2 * ROWS) + cc * ROWS + low, 32)
        return w.at[zz * 2 + lax.div(yy, 2), pl.ds(start, count), :]

    def span(index, size, count=None):
        return pl.ds(pl.multiple_of(index * size, size), size if count is None else count)

    barrier = pltpu.get_barrier_semaphore()
    peers = [member_device(i)[1] for i in range(1, 16)]
    peers += [sub_device(i)[1] for i in range(1, 8)]
    peers += [device(z, ya, c, x)]
    for peer in peers:
        pl.semaphore_signal(barrier, inc=1, device_id=peer, device_id_type=MESH)

    loads = [
        (master_hbm.at[:, span(half, COLS)], master_own),
        (master_hbm.at[:, span(1 - half, COLS)], master_far),
        (embed_hbm, emb),
        (readout_hbm.at[span(half, COLS), :], ro),
        (target_hbm, tgt),
    ]
    loads = [pltpu.make_async_copy(a, b, local_sem.at[i]) for i, (a, b) in enumerate(loads)]
    for load in loads:
        load.start()

    def as_row(ref):
        return jnp.concatenate([ref[i : i + 1, :] for i in range(SLOTS // 128)], axis=1)

    group, offset = as_row(group_row), as_row(offset_row)
    live = iota((1, SLOTS), 1) < row_count[0]
    to_member = (group >> 3) * 4 + ((group >> 2) & 1) * 2 + (group & 1)
    block = sum((offset >= BLOCK * i).astype(i32) for i in range(1, 4))
    place = offset - block * BLOCK + 1
    to_sub = ((group >> 1) & 1) * 4 + block
    key = jnp.where(live, to_member * 8 + to_sub, -1)
    row_id, col_id = iota((SLOTS, SLOTS), 0), iota((SLOTS, SLOTS), 1)

    def column(values):
        wide = jnp.broadcast_to(values.astype(f32), (SLOTS, SLOTS))
        return jnp.sum(jnp.where(row_id == col_id, wide, 0.0), axis=1, keepdims=True)

    same = (column(key) == key.astype(f32)) & (row_id < col_id)
    rank = jnp.sum(jnp.where(same, 1.0, 0.0), axis=0, keepdims=True).astype(i32)
    slot = jnp.where(live, to_member * 32 + rank * 8 + to_sub, -1)
    pick = jnp.where(iota((512, SLOTS), 0) == slot, 1.0, 0.0).astype(bf16)
    marks = jnp.broadcast_to(column(place), (SLOTS, 128)).astype(bf16)
    out1[:, :128] = matmul(pick, patches[...]).astype(bf16)
    out1[:, 128:] = matmul(pick, marks).astype(bf16)

    loads[0].wait()
    loads[1].wait()
    own = chunk(z, y, c)
    own[...] = master_own[...].astype(bf16)
    far_half[...] = master_far[...].astype(bf16)

    pl.semaphore_wait(barrier, len(peers))

    sends = []

    def launch(copy):
        copy.start()
        sends.append(copy)

    for i in range(1, 16):
        other, to = member_device(i)
        launch(
            remote(
                out1.at[span(other, 32), :],
                in1.at[span(member, 32), :],
                r1_send.at[other],
                r1_recv.at[member],
                to,
            )
        )

    def gather(event, src, dst, to):
        remote(src, dst, ag_send.at[event], ag_recv.at[event], to).start()

    def gathered(event, dst):
        remote(dst, dst, ag_send.at[event], ag_recv.at[event], device(z, y, oc, x)).wait_recv()

    def along_z(event, zz, yy, low=0, count=ROWS, up=True):
        piece = chunk(zz, yy, c, low, count)
        gather(event, piece, piece, device(zp if up else zm, y, c, x))

    def full_z(event, yy):
        along_z(event, z, yy)
        along_z(event + 1, z, yy, up=False)

    def halves_z(event, yy):
        along_z(event + 2, zm, yy, 0, ROWS // 2)
        along_z(event + 3, zp, yy, ROWS // 2, ROWS // 2, up=False)

    def wait_full(event, yy):
        gathered(event, chunk(zm, yy, c))
        gathered(event + 1, chunk(zp, yy, c))

    def wait_halves(event, yy):
        gathered(event + 2, chunk(z2, yy, c, 0, ROWS // 2))
        gathered(event + 3, chunk(z2, yy, c, ROWS // 2, ROWS // 2))

    def along_y(j):
        piece = chunk(zs[j], yp, c)
        gather(14 + j, piece, piece, device(z, ya, c, x))

    def wait_y(j):
        gathered(14 + j, chunk(zs[j], yap, c))

    def relay(j, l):
        piece = chunk(zs[j], ys[l], c)
        gather(18 + j * 4 + l, piece, piece, device(z, y, oc, x))

    def wait_relay(j, l):
        gathered(18 + j * 4 + l, chunk(zs[j], ys[l], oc))

    gather(0, far_half, own, device(z, yp, c, x))
    gather(1, own, own, device(z, ya, c, x))
    full_z(2, y)
    relay(0, 0)

    gains = gain[...].astype(f32)
    lanes = COLS // 128
    for j in range(8):
        rows = [gains[lanes * j + l : lanes * j + l + 1] for l in range(lanes)]
        gain_rows[j] = jnp.concatenate(rows, axis=1)
    ssq[...] = jnp.zeros_like(ssq)
    acc[...] = jnp.zeros_like(acc)
    in1[span(member, 32), :] = out1[span(member, 32), :]
    row512 = iota((512, 512), 0)
    source = (row512 & 15) * 32 + ((row512 >> 4) & 3) * 8 + (row512 >> 6)
    perm[...] = jnp.where(iota((512, 512), 1) == source, 1.0, 0.0).astype(bf16)
    for i in range(1, 16):
        other, to = member_device(i)
        landed = in1.at[span(other, 32), :]
        remote(landed, landed, r1_send.at[other], r1_recv.at[other], to).wait_recv()
    out2[...] = matmul(perm[...], in1[...]).astype(bf16)
    for i in range(1, 8):
        other, to = sub_device(i)
        launch(
            remote(
                out2.at[span(other, 64, 48), :],
                in2.at[span(sub, 48), :],
                r2_send.at[other],
                r2_recv.at[sub],
                to,
            )
        )
    in2[span(sub, 48), :] = out2[span(sub, 64, 48), :]

    gathered(0, chunk(z, yp, c))
    full_z(10, yp)
    along_y(0)
    relay(0, 1)

    for i in range(1, 8):
        other, to = sub_device(i)
        landed = in2.at[span(other, 48), :]
        remote(landed, landed, r2_send.at[other], r2_recv.at[other], to).wait_recv()
    mark = in2[:, 128:].astype(f32)
    lane = iota((SLOTS, 128), 1)
    to_place = jnp.concatenate(
        [
            jnp.where(mark == (lane + 1).astype(f32), 1.0, 0.0),
            jnp.where(mark == (lane + 129).astype(f32), 1.0, 0.0),
        ],
        axis=1,
    ).astype(bf16)
    mine = span(sub, BLOCK)
    batch[mine, :] = matmul(to_place, in2[:, :128], TN)[:BLOCK].astype(bf16)
    for i in range(1, 8):
        other, to = sub_device(i)
        launch(remote(batch.at[mine, :], batch.at[mine, :], r3_send.at[other], r3_recv.at[sub], to))

    wait_full(2, y)
    relay(1, 0)
    relay(2, 0)
    gathered(1, chunk(z, ya, c))
    relay(0, 2)
    wait_full(10, yp)
    along_y(1)
    along_y(2)
    halves_z(10, yp)
    full_z(6, ya)
    relay(1, 1)
    relay(2, 1)

    for i in range(1, 8):
        other, to = sub_device(i)
        landed = batch.at[span(other, BLOCK), :]
        remote(landed, landed, r3_send.at[other], r3_recv.at[other], to).wait_recv()
    loads[2].wait()

    def embed(j, carry):
        @pl.when(j == 3)
        def _():
            wait_halves(10, yp)
            halves_z(2, y)
            relay(3, 1)
            wait_y(0)
            relay(0, 3)

        @pl.when(j == 6)
        def _():
            wait_full(6, ya)
            halves_z(6, ya)
            relay(1, 2)
            relay(2, 2)

        v = matmul(batch[...], emb[:, span(j, COLS)])
        t = jnp.tanh(v * (gelu_const + (gelu_const * cubic) * (v * v)))
        twice = v + v * t
        square = twice * twice
        total = sum(square[:, l * 128 : (l + 1) * 128] for l in range(COLS // 128))
        ssq[...] += total
        hg[j] = (twice * gain_rows[j]).astype(bf16)
        return carry

    lax.fori_loop(0, 8, embed, 0)

    def forward(i, carry):
        @pl.when(i == 0)
        def _():
            for l in range(2):
                wait_relay(0, l)

        @pl.when(i == 1)
        def _():
            for l in range(2, 4):
                wait_relay(0, l)

        @pl.when(i == 2)
        def _():
            for l in range(2):
                wait_relay(1, l)

        @pl.when(i == 3)
        def _():
            wait_y(1)
            along_y(3)
            relay(1, 3)
            wait_halves(2, y)
            relay(3, 0)
            for l in range(2, 4):
                wait_relay(1, l)

        @pl.when(i == 4)
        def _():
            wait_y(2)
            relay(2, 3)
            for l in range(2):
                wait_relay(2, l)

        @pl.when(i == 5)
        def _():
            wait_halves(6, ya)
            relay(3, 2)
            for l in range(2, 4):
                wait_relay(2, l)

        @pl.when(i == 6)
        def _():
            for l in range(2):
                wait_relay(3, l)

        @pl.when(i == 7)
        def _():
            wait_y(3)
            relay(3, 3)
            for l in range(2, 4):
                wait_relay(3, l)

        j, far = lax.div(i, 2), lax.rem(i, 2)
        zz = lax.rem(z + j + lax.div(j, 2) - 2 * lax.div(j, 3), 4)
        g = zz * 2 + k + far * (1 - 2 * k)
        acc[...] += matmul(hg[g], w[g])
        return carry

    lax.fori_loop(0, 8, forward, 0)

    loads[3].wait()
    loads[4].wait()

    def row_scale(rows):
        mean4 = jnp.sum(ssq[rows, :], axis=1, keepdims=True) * (0.25 / WIDTH)
        return lax.rsqrt(mean4 + 1e-05) * (0.5 * SCALE)

    def partial(index):
        rows = span(index, BLOCK)
        v = acc[rows, :] * row_scale(rows)
        t = jnp.tanh(v * (gelu_const + (gelu_const * cubic) * (v * v)))
        return matmul((0.5 * v * (1.0 + t)).astype(bf16), ro[...])

    for i in range(1, 8):
        other, to = sub_device(i)
        part_out[other] = partial(other).astype(bf16)
        launch(
            remote(part_out.at[other], part_in.at[sub], part_send.at[other], part_recv.at[sub], to)
        )
    part_own[...] = partial(sub)

    def slope(i, carry):
        rows = span(i, BLOCK)
        r = row_scale(rows)
        v = acc[rows, :] * r
        t = jnp.tanh(v * (gelu_const + (gelu_const * cubic) * (v * v)))
        acc[rows, :] = r * (
            0.5 * (1.0 + t)
            + (0.5 * gelu_const) * v * (1.0 - t * t) * (1.0 + (3.0 * cubic) * (v * v))
        )
        return carry

    lax.fori_loop(0, 8, slope, 0)
    total = part_own[...]
    for i in range(1, 8):
        other, to = sub_device(i)
        landed = part_in.at[other]
        remote(landed, landed, part_send.at[other], part_recv.at[other], to).wait_recv()
        total = total + part_in[other].astype(f32)
    total = total.astype(bf16)
    err_in[sub] = total
    err_own[...] = (total.astype(f32) - tgt[span(x, BLOCK), :].astype(f32)).astype(bf16)
    for i in range(4):
        other = lax.rem(x + i, 4)
        launch(
            remote(
                err_own,
                err_in.at[sub],
                err_send.at[(1 - p) * 4 + other],
                err_recv.at[sub],
                device(z, yp, c, other),
            )
        )
        if i:
            launch(
                remote(
                    err_in.at[sub],
                    err_in.at[sub],
                    err_send.at[p * 4 + other],
                    err_recv.at[sub],
                    device(z, y, c, other),
                )
            )

    def backward(index, errors):
        rows = span(index, BLOCK)
        delta[rows, :] = (matmul(errors, ro[...], NT) * acc[rows, :]).astype(bf16)

    for i in range(4):
        other = lax.rem(x + i, 4)
        index = p * 4 + other
        landed = err_in.at[index]
        if i:
            to = device(z, y, c, other)
            remote(landed, landed, err_send.at[index], err_recv.at[index], to).wait_recv()
        rows = span(other, BLOCK)
        pred_out[rows, :] = err_in[index]
        backward(index, (err_in[index].astype(f32) - tgt[rows, :].astype(f32)).astype(bf16))
    for i in range(4):
        other = lax.rem(x + i, 4)
        index = (1 - p) * 4 + other
        landed = err_in.at[index]
        to = device(z, yp, c, other)
        remote(landed, landed, err_send.at[index], err_recv.at[index], to).wait_recv()
        backward(index, err_in[index])

    for event in range(34):
        piece = far_half.at[: ROWS // 2, :] if event in (4, 5, 8, 9, 12, 13) else far_half
        to = device(z, y, oc, x)
        remote(piece, piece, ag_send.at[event], ag_recv.at[event], to).wait_send()

    def scatter(event, src, dst, to):
        launch(remote(src, dst, rs_send.at[event], rs_recv.at[event], to))

    def scattered(event, dst):
        remote(dst, dst, rs_send.at[event], rs_recv.at[event], device(z, y, oc, x)).wait_recv()

    def add(target, terms, count=ROWS):
        def tile(i, carry):
            rows = span(i, 48)
            value = target[rows, :].astype(f32)
            for term in terms:
                value = value + term[rows, :].astype(f32)
            target[rows, :] = value.astype(bf16)
            return carry

        lax.fori_loop(0, count // 48, tile, 0)

    def core_slot(zz, yy):
        start = pl.multiple_of(lax.rem(yy, 2) * ROWS, 32)
        return core_in.at[zz * 2 + lax.div(yy, 2), pl.ds(start, ROWS), :]

    def gradient(j, far):
        zz = zs[j]
        g = zz * 2 + (kk if far else k)


        def tile(i, carry):
            rows = span(i, 384)
            w[g, rows, :] = matmul(hg[g, :, rows], delta[...], TN).astype(bf16)
            return carry

        lax.fori_loop(0, 2, tile, 0)
        for l in (3, 2) if far else (0, 1):
            scatter(j * 4 + l, chunk(zz, ys[l], oc), core_slot(zz, ys[l]), device(z, y, oc, x))

    def cores(j, l):
        scattered(j * 4 + l, core_slot(zs[j], ys[l]))
        add(chunk(zs[j], ys[l], c), [core_slot(zs[j], ys[l])])

    kinds = {0: y, 1: ya, 2: yp}
    down, up = device(zm, y, c, x), device(zp, y, c, x)

    def send_halves(kind):
        yy = kinds[kind]
        event = 16 + 4 * kind
        scatter(event, chunk(z2, yy, c, 0, ROWS // 2), zhalf_in.at[kind, 0], down)
        scatter(event + 1, chunk(z2, yy, c, ROWS // 2, ROWS // 2), zhalf_in.at[kind, 1], up)

    def send_full(kind, side):
        yy = kinds[kind]
        event = 16 + 4 * kind + side
        zz = (zm, zp)[side]
        scattered(event, zhalf_in.at[kind, side])
        add(
            chunk(zz, yy, c, side * (ROWS // 2), ROWS // 2),
            [zhalf_in.at[kind, side]],
            ROWS // 2,
        )
        scatter(event + 2, chunk(zz, yy, c), zfull_in.at[kind, side], (down, up)[side])

    def wait_fulls(kind):
        for side in range(2):
            scattered(18 + 4 * kind + side, zfull_in.at[kind, side])
        return [zfull_in.at[kind, side] for side in range(2)]

    def send_y(j):
        scatter(28 + j, chunk(zs[j], yap, c), y_in.at[j], device(z, ya, c, x))

    def take_y(j):
        scattered(28 + j, y_in.at[j])
        add(chunk(zs[j], yp, c), [y_in.at[j]])

    gradient(3, True)
    cores(3, 3)
    send_y(3)
    cores(3, 2)
    send_halves(1)
    gradient(3, False)
    cores(3, 0)
    send_halves(0)
    gradient(1, True)
    cores(1, 3)
    send_y(1)
    cores(3, 1)
    gradient(2, True)
    cores(2, 3)
    send_y(2)
    take_y(3)
    send_halves(2)
    cores(1, 2)
    send_full(1, 1)
    cores(2, 2)
    send_full(1, 0)
    gradient(1, False)
    cores(1, 0)
    send_full(0, 1)
    gradient(2, False)
    cores(2, 0)
    send_full(0, 0)
    gradient(0, True)
    cores(0, 3)
    send_y(0)
    gradient(0, False)
    cores(1, 1)
    cores(2, 1)
    cores(0, 2)
    take_y(1)
    send_full(2, 1)
    take_y(2)
    send_full(2, 0)
    add(chunk(z, ya, c), wait_fulls(1))
    scatter(32, chunk(z, ya, c), y_in.at[4], device(z, ya, c, x))
    cores(0, 1)
    cores(0, 0)
    take_y(0)
    add(chunk(z, yp, c), wait_fulls(2))
    scatter(33, chunk(z, yp, c), pair_in, device(z, yp, c, x))
    terms = wait_fulls(0)
    scattered(32, y_in.at[4])
    terms = terms + [y_in.at[4]]

    def finish(i, carry):
        rows = span(i, 48)
        value = own[rows, :].astype(f32)
        for term in terms:
            value = value + term[rows, :].astype(f32)
        grad_out[rows, span(half, COLS)] = value
        return carry

    lax.fori_loop(0, ROWS // 48, finish, 0)
    scattered(33, pair_in)
    grad_out[:, span(1 - half, COLS)] = pair_in[...].astype(f32)
    for copy in sends:
        copy.wait_send()


def step(row_count, patches, group, offset, gain, embed, readout, target, master):
    vmem = pl.BlockSpec(memory_space=pltpu.VMEM)
    smem = pl.BlockSpec(memory_space=pltpu.SMEM)
    hbm = pl.BlockSpec(memory_space=pl.ANY)
    dma = pltpu.SemaphoreType.DMA
    return pl.pallas_call(
        kernel,
        out_shape=(
            jax.ShapeDtypeStruct((640, 128), bf16),
            jax.ShapeDtypeStruct((ROWS, 2 * COLS), f32),
        ),
        in_specs=[smem, vmem, vmem, vmem, vmem, hbm, hbm, hbm, hbm],
        out_specs=(vmem, vmem),
        scratch_shapes=[
            pltpu.VMEM((128, WIDTH), bf16),
            pltpu.VMEM((COLS, 128), bf16),
            pltpu.VMEM((640, 128), bf16),
            pltpu.VMEM((ROWS, COLS), f32),
            pltpu.VMEM((ROWS, COLS), f32),
            pltpu.VMEM((ROWS, COLS), bf16),
            pltpu.VMEM((8, COLS, COLS), bf16),
            pltpu.VMEM((8, TOKENS, COLS), bf16),
            pltpu.VMEM((TOKENS, COLS), f32),
            pltpu.VMEM((TOKENS, COLS), bf16),
            pltpu.VMEM((TOKENS, 128), f32),
            pltpu.VMEM((8, 1, COLS), f32),
            pltpu.VMEM((512, 512), bf16),
            pltpu.VMEM((512, 256), bf16),
            pltpu.VMEM((512, 256), bf16),
            pltpu.VMEM((512, 256), bf16),
            pltpu.VMEM((SLOTS, 256), bf16),
            pltpu.VMEM((TOKENS, 128), bf16),
            pltpu.VMEM((8, BLOCK, 128), bf16),
            pltpu.VMEM((8, BLOCK, 128), bf16),
            pltpu.VMEM((BLOCK, 128), f32),
            pltpu.VMEM((BLOCK, 128), bf16),
            pltpu.VMEM((8, BLOCK, 128), bf16),
            pltpu.VMEM((8, 2 * ROWS, COLS), bf16),
            pltpu.VMEM((3, 2, ROWS // 2, COLS), bf16),
            pltpu.VMEM((3, 2, ROWS, COLS), bf16),
            pltpu.VMEM((5, ROWS, COLS), bf16),
            pltpu.VMEM((ROWS, COLS), bf16),
            dma((5,)),
            dma((16,)),
            dma((16,)),
            dma((8,)),
            dma((8,)),
            dma((8,)),
            dma((8,)),
            dma((34,)),
            dma((34,)),
            dma((8,)),
            dma((8,)),
            dma((8,)),
            dma((8,)),
            dma((34,)),
            dma((34,)),
        ],
        compiler_params=pltpu.CompilerParams(
            collective_id=0, has_side_effects=True, vmem_limit_bytes=56 * 1024 * 1024
        ),
        name="train_step",
    )(row_count, patches, group, offset, gain, embed, readout, target, master)


def shards(
    patches,
    row_count,
    target_group,
    target_offset,
    embed,
    norm_gain,
    readout,
    target,
    master,
    moment1,
    moment2,
):
    prediction, gradient = step(
        row_count,
        patches,
        target_group.reshape(3, 128),
        target_offset.reshape(3, 128),
        norm_gain.reshape(48, 128),
        embed,
        readout,
        target,
        master,
    )
    moment1_new = beta_one * moment1 + (1.0 - beta_one) * gradient
    moment2_new = beta_two * moment2 + (1.0 - beta_two) * gradient * gradient
    first_fix = moment1_new / (1.0 - beta_one**step_count)
    second_fix = moment2_new / (1.0 - beta_two**step_count)
    master_new = master - learn_rate * (
        first_fix / (jnp.sqrt(second_fix) + adam_epsilon) + decay_rate * master
    )
    return (
        prediction.astype(f32),
        master_new,
        moment1_new,
        moment2_new,
        master_new.astype(bf16),
    )


def solution(mesh):
    placed = (
        P(("dp", "mp"), None),
        P(("dp", "mp")),
        P(("dp", "mp")),
        P(("dp", "mp")),
        P(),
        P(),
        P("mp", None),
        P("dp", None),
        P("dp", "mp"),
        P("dp", "mp"),
        P("dp", "mp"),
    )
    return jax.shard_map(
        shards,
        mesh=mesh,
        in_specs=placed,
        out_specs=(P("dp", None), P("dp", "mp"), P("dp", "mp"), P("dp", "mp"), P("dp", "mp")),
        check_vma=False,
    )
```

```python
import jax
import jax.numpy as jnp
from jax import lax
from jax.experimental import pallas as pl
from jax.experimental.pallas import tpu as pltpu
from jax.sharding import PartitionSpec as P

gelu_const = 0.7978845608028654
cubic = 0.044715
beta_one = 0.9
beta_two = 0.95
learn_rate = 0.01
decay_rate = 0.1
adam_epsilon = 1e-08
step_count = 20

WIDTH = 6144
ROWS = 192
COLS = 768
TOKENS = 1280
BLOCK = 160
SLOTS = 384
SCALE = 1.0 / WIDTH**0.5
MESH = pl.DeviceIdType.MESH
f32, bf16, i32 = jnp.float32, jnp.bfloat16, jnp.int32

NN = (((1,), (0,)), ((), ()))
NT = (((1,), (1,)), ((), ()))
TN = (((0,), (0,)), ((), ()))


def matmul(a, b, dims=NN):
    return lax.dot_general(a, b, dims, preferred_element_type=f32)


def iota(shape, axis):
    return lax.broadcasted_iota(i32, shape, axis)


def kernel(
    row_count,
    patches,
    group_row,
    offset_row,
    gain,
    embed_hbm,
    readout_hbm,
    target_hbm,
    master_hbm,
    pred_out,
    grad_out,
    emb,
    ro,
    tgt,
    master_own,
    master_far,
    far_half,
    w,
    hg,
    acc,
    delta,
    ssq,
    gain_rows,
    perm,
    out1,
    in1,
    out2,
    in2,
    batch,
    part_out,
    part_in,
    part_own,
    err_own,
    err_in,
    core_in,
    zhalf_in,
    zfull_in,
    y_in,
    pair_in,
    local_sem,
    r1_send,
    r1_recv,
    r2_send,
    r2_recv,
    r3_send,
    r3_recv,
    ag_send,
    ag_recv,
    part_send,
    part_recv,
    err_send,
    err_recv,
    rs_send,
    rs_recv,
):
    dp, x = lax.axis_index("dp"), lax.axis_index("mp")
    z = lax.div(dp, 8)
    y = lax.rem(lax.div(dp, 2), 4)
    c = lax.rem(dp, 2)
    k = lax.div(y, 2)
    p = lax.rem(y, 2)
    half = lax.rem(p + k, 2)
    yp = y + 1 - 2 * p
    ya = 3 - y
    yap = 3 - yp
    kk, oc = 1 - k, 1 - c
    zp, zm, z2 = lax.rem(z + 1, 4), lax.rem(z + 3, 4), lax.rem(z + 2, 4)
    member = z * 4 + k * 2 + c
    sub = p * 4 + x
    zs = (z, zp, zm, z2)
    ys = (y, yp, ya, yap)

    def device(zz, yy, cc, xx):
        return ((zz * 4 + yy) * 2 + cc, xx)

    def member_device(i):
        other = lax.rem(member + i, 16)
        zz, kz, cc = lax.div(other, 4), lax.rem(lax.div(other, 2), 2), lax.rem(other, 2)
        return other, device(zz, 2 * kz + p, cc, x)

    def sub_device(i):
        other = lax.rem(sub + i, 8)
        return other, device(z, 2 * k + lax.div(other, 4), c, lax.rem(other, 4))

    def remote(src, dst, send, recv, to):
        return pltpu.make_async_remote_copy(
            src_ref=src, dst_ref=dst, send_sem=send, recv_sem=recv, device_id=to, device_id_type=MESH
        )

    def chunk(zz, yy, cc, low=0, count=ROWS):
        start = pl.multiple_of(lax.rem(yy, 2) * (2 * ROWS) + cc * ROWS + low, 32)
        return w.at[zz * 2 + lax.div(yy, 2), pl.ds(start, count), :]

    def span(index, size, count=None):
        return pl.ds(pl.multiple_of(index * size, size), size if count is None else count)

    barrier = pltpu.get_barrier_semaphore()
    peers = [member_device(i)[1] for i in range(1, 16)]
    peers += [sub_device(i)[1] for i in range(1, 8)]
    peers += [device(z, ya, c, x)]
    for peer in peers:
        pl.semaphore_signal(barrier, inc=1, device_id=peer, device_id_type=MESH)

    loads = [
        (master_hbm.at[:, span(half, COLS)], master_own),
        (master_hbm.at[:, span(1 - half, COLS)], master_far),
        (embed_hbm, emb),
        (readout_hbm.at[span(half, COLS), :], ro),
        (target_hbm, tgt),
    ]
    loads = [pltpu.make_async_copy(a, b, local_sem.at[i]) for i, (a, b) in enumerate(loads)]
    for load in loads:
        load.start()

    def as_row(ref):
        return jnp.concatenate([ref[i : i + 1, :] for i in range(SLOTS // 128)], axis=1)

    group, offset = as_row(group_row), as_row(offset_row)
    live = iota((1, SLOTS), 1) < row_count[0]
    to_member = (group >> 3) * 4 + ((group >> 2) & 1) * 2 + (group & 1)
    block = sum((offset >= BLOCK * i).astype(i32) for i in range(1, 4))
    place = offset - block * BLOCK + 1
    to_sub = ((group >> 1) & 1) * 4 + block
    key = jnp.where(live, to_member * 8 + to_sub, -1)
    row_id, col_id = iota((SLOTS, SLOTS), 0), iota((SLOTS, SLOTS), 1)

    def column(values):
        wide = jnp.broadcast_to(values.astype(f32), (SLOTS, SLOTS))
        return jnp.sum(jnp.where(row_id == col_id, wide, 0.0), axis=1, keepdims=True)

    same = (column(key) == key.astype(f32)) & (row_id < col_id)
    rank = jnp.sum(jnp.where(same, 1.0, 0.0), axis=0, keepdims=True).astype(i32)
    slot = jnp.where(live, to_member * 32 + rank * 8 + to_sub, -1)
    pick = jnp.where(iota((512, SLOTS), 0) == slot, 1.0, 0.0).astype(bf16)
    marks = jnp.broadcast_to(column(place), (SLOTS, 128)).astype(bf16)
    out1[:, :128] = matmul(pick, patches[...]).astype(bf16)
    out1[:, 128:] = matmul(pick, marks).astype(bf16)

    loads[0].wait()
    loads[1].wait()
    own = chunk(z, y, c)
    own[...] = master_own[...].astype(bf16)
    far_half[...] = master_far[...].astype(bf16)

    pl.semaphore_wait(barrier, len(peers))

    sends = []

    def launch(copy):
        copy.start()
        sends.append(copy)

    for i in range(1, 16):
        other, to = member_device(i)
        launch(
            remote(
                out1.at[span(other, 32), :],
                in1.at[span(member, 32), :],
                r1_send.at[other],
                r1_recv.at[member],
                to,
            )
        )

    def gather(event, src, dst, to):
        remote(src, dst, ag_send.at[event], ag_recv.at[event], to).start()

    def gathered(event, dst):
        remote(dst, dst, ag_send.at[event], ag_recv.at[event], device(z, y, oc, x)).wait_recv()

    def along_z(event, zz, yy, low=0, count=ROWS, up=True):
        piece = chunk(zz, yy, c, low, count)
        gather(event, piece, piece, device(zp if up else zm, y, c, x))

    def full_z(event, yy):
        along_z(event, z, yy)
        along_z(event + 1, z, yy, up=False)

    def halves_z(event, yy):
        along_z(event + 2, zm, yy, 0, ROWS // 2)
        along_z(event + 3, zp, yy, ROWS // 2, ROWS // 2, up=False)

    def wait_full(event, yy):
        gathered(event, chunk(zm, yy, c))
        gathered(event + 1, chunk(zp, yy, c))

    def wait_halves(event, yy):
        gathered(event + 2, chunk(z2, yy, c, 0, ROWS // 2))
        gathered(event + 3, chunk(z2, yy, c, ROWS // 2, ROWS // 2))

    def along_y(j):
        piece = chunk(zs[j], yp, c)
        gather(14 + j, piece, piece, device(z, ya, c, x))

    def wait_y(j):
        gathered(14 + j, chunk(zs[j], yap, c))

    def relay(j, l):
        piece = chunk(zs[j], ys[l], c)
        gather(18 + j * 4 + l, piece, piece, device(z, y, oc, x))

    def wait_relay(j, l):
        gathered(18 + j * 4 + l, chunk(zs[j], ys[l], oc))

    gather(0, far_half, own, device(z, yp, c, x))
    gather(1, own, own, device(z, ya, c, x))
    full_z(2, y)
    relay(0, 0)

    gains = gain[...].astype(f32)
    lanes = COLS // 128
    for j in range(8):
        rows = [gains[lanes * j + l : lanes * j + l + 1] for l in range(lanes)]
        gain_rows[j] = jnp.concatenate(rows, axis=1)
    ssq[...] = jnp.zeros_like(ssq)
    acc[...] = jnp.zeros_like(acc)
    in1[span(member, 32), :] = out1[span(member, 32), :]
    row512 = iota((512, 512), 0)
    source = (row512 & 15) * 32 + ((row512 >> 4) & 3) * 8 + (row512 >> 6)
    perm[...] = jnp.where(iota((512, 512), 1) == source, 1.0, 0.0).astype(bf16)
    for i in range(1, 16):
        other, to = member_device(i)
        landed = in1.at[span(other, 32), :]
        remote(landed, landed, r1_send.at[other], r1_recv.at[other], to).wait_recv()
    out2[...] = matmul(perm[...], in1[...]).astype(bf16)
    for i in range(1, 8):
        other, to = sub_device(i)
        launch(
            remote(
                out2.at[span(other, 64, 48), :],
                in2.at[span(sub, 48), :],
                r2_send.at[other],
                r2_recv.at[sub],
                to,
            )
        )
    in2[span(sub, 48), :] = out2[span(sub, 64, 48), :]

    gathered(0, chunk(z, yp, c))
    full_z(10, yp)
    along_y(0)
    relay(0, 1)

    for i in range(1, 8):
        other, to = sub_device(i)
        landed = in2.at[span(other, 48), :]
        remote(landed, landed, r2_send.at[other], r2_recv.at[other], to).wait_recv()
    mark = in2[:, 128:].astype(f32)
    lane = iota((SLOTS, 128), 1)
    to_place = jnp.concatenate(
        [
            jnp.where(mark == (lane + 1).astype(f32), 1.0, 0.0),
            jnp.where(mark == (lane + 129).astype(f32), 1.0, 0.0),
        ],
        axis=1,
    ).astype(bf16)
    mine = span(sub, BLOCK)
    batch[mine, :] = matmul(to_place, in2[:, :128], TN)[:BLOCK].astype(bf16)
    for i in range(1, 8):
        other, to = sub_device(i)
        launch(remote(batch.at[mine, :], batch.at[mine, :], r3_send.at[other], r3_recv.at[sub], to))

    wait_full(2, y)
    relay(1, 0)
    relay(2, 0)
    gathered(1, chunk(z, ya, c))
    relay(0, 2)
    wait_full(10, yp)
    along_y(1)
    along_y(2)
    halves_z(10, yp)
    full_z(6, ya)
    relay(1, 1)
    relay(2, 1)

    for i in range(1, 8):
        other, to = sub_device(i)
        landed = batch.at[span(other, BLOCK), :]
        remote(landed, landed, r3_send.at[other], r3_recv.at[other], to).wait_recv()
    loads[2].wait()

    def embed(j, carry):
        @pl.when(j == 3)
        def _():
            wait_halves(10, yp)
            halves_z(2, y)
            relay(3, 1)
            wait_y(0)
            relay(0, 3)

        @pl.when(j == 5)
        def _():
            along_y(3)
            wait_full(6, ya)
            halves_z(6, ya)
            relay(1, 2)
            relay(2, 2)

        v = matmul(batch[...], emb[:, span(j, COLS)])
        t = jnp.tanh(v * (gelu_const + (gelu_const * cubic) * (v * v)))
        twice = v + v * t
        square = twice * twice
        total = sum(square[:, l * 128 : (l + 1) * 128] for l in range(COLS // 128))
        ssq[...] += total
        hg[j] = (twice * gain_rows[j]).astype(bf16)
        return carry

    lax.fori_loop(0, 8, embed, 0)

    def forward(i, carry):
        @pl.when(i == 0)
        def _():
            for l in range(2):
                wait_relay(0, l)

        @pl.when(i == 1)
        def _():
            for l in range(2, 4):
                wait_relay(0, l)

        @pl.when(i == 2)
        def _():
            for l in range(2):
                wait_relay(1, l)

        @pl.when(i == 3)
        def _():
            wait_y(1)
            relay(1, 3)
            wait_halves(2, y)
            relay(3, 0)
            for l in range(2, 4):
                wait_relay(1, l)

        @pl.when(i == 4)
        def _():
            wait_y(2)
            relay(2, 3)
            for l in range(2):
                wait_relay(2, l)

        @pl.when(i == 5)
        def _():
            wait_halves(6, ya)
            relay(3, 2)
            for l in range(2, 4):
                wait_relay(2, l)

        @pl.when(i == 6)
        def _():
            for l in range(2):
                wait_relay(3, l)

        @pl.when(i == 7)
        def _():
            wait_y(3)
            relay(3, 3)
            for l in range(2, 4):
                wait_relay(3, l)

        j, far = lax.div(i, 2), lax.rem(i, 2)
        zz = lax.rem(z + j + lax.div(j, 2) - 2 * lax.div(j, 3), 4)
        g = zz * 2 + k + far * (1 - 2 * k)
        acc[...] += matmul(hg[g], w[g])
        return carry

    lax.fori_loop(0, 8, forward, 0)

    loads[3].wait()
    loads[4].wait()

    def row_scale(rows):
        mean4 = jnp.sum(ssq[rows, :], axis=1, keepdims=True) * (0.25 / WIDTH)
        return lax.rsqrt(mean4 + 1e-05) * (0.5 * SCALE)

    def partial(index):
        rows = span(index, BLOCK)
        v = acc[rows, :] * row_scale(rows)
        t = jnp.tanh(v * (gelu_const + (gelu_const * cubic) * (v * v)))
        return matmul((0.5 * v * (1.0 + t)).astype(bf16), ro[...])

    for i in range(1, 8):
        other, to = sub_device(i)
        part_out[other] = partial(other).astype(bf16)
        launch(
            remote(part_out.at[other], part_in.at[sub], part_send.at[other], part_recv.at[sub], to)
        )
    part_own[...] = partial(sub)

    def slope(i, carry):
        rows = span(i, BLOCK)
        r = row_scale(rows)
        v = acc[rows, :] * r
        t = jnp.tanh(v * (gelu_const + (gelu_const * cubic) * (v * v)))
        acc[rows, :] = r * (
            0.5 * (1.0 + t)
            + (0.5 * gelu_const) * v * (1.0 - t * t) * (1.0 + (3.0 * cubic) * (v * v))
        )
        return carry

    lax.fori_loop(0, 8, slope, 0)
    total = part_own[...]
    for i in range(1, 8):
        other, to = sub_device(i)
        landed = part_in.at[other]
        remote(landed, landed, part_send.at[other], part_recv.at[other], to).wait_recv()
        total = total + part_in[other].astype(f32)
    total = total.astype(bf16)
    err_in[sub] = total
    err_own[...] = (total.astype(f32) - tgt[span(x, BLOCK), :].astype(f32)).astype(bf16)
    for i in range(4):
        other = lax.rem(x + i, 4)
        launch(
            remote(
                err_own,
                err_in.at[sub],
                err_send.at[(1 - p) * 4 + other],
                err_recv.at[sub],
                device(z, yp, c, other),
            )
        )
        if i:
            launch(
                remote(
                    err_in.at[sub],
                    err_in.at[sub],
                    err_send.at[p * 4 + other],
                    err_recv.at[sub],
                    device(z, y, c, other),
                )
            )

    def backward(index, errors):
        rows = span(index, BLOCK)
        delta[rows, :] = (matmul(errors, ro[...], NT) * acc[rows, :]).astype(bf16)

    for i in range(4):
        other = lax.rem(x + i, 4)
        index = p * 4 + other
        landed = err_in.at[index]
        if i:
            to = device(z, y, c, other)
            remote(landed, landed, err_send.at[index], err_recv.at[index], to).wait_recv()
        rows = span(other, BLOCK)
        pred_out[rows, :] = err_in[index]
        backward(index, (err_in[index].astype(f32) - tgt[rows, :].astype(f32)).astype(bf16))
    for i in range(4):
        other = lax.rem(x + i, 4)
        index = (1 - p) * 4 + other
        landed = err_in.at[index]
        to = device(z, yp, c, other)
        remote(landed, landed, err_send.at[index], err_recv.at[index], to).wait_recv()
        backward(index, err_in[index])

    for event in range(34):
        piece = far_half.at[: ROWS // 2, :] if event in (4, 5, 8, 9, 12, 13) else far_half
        to = device(z, y, oc, x)
        remote(piece, piece, ag_send.at[event], ag_recv.at[event], to).wait_send()

    def scatter(event, src, dst, to):
        launch(remote(src, dst, rs_send.at[event], rs_recv.at[event], to))

    def scattered(event, dst):
        remote(dst, dst, rs_send.at[event], rs_recv.at[event], device(z, y, oc, x)).wait_recv()

    def add(target, terms, count=ROWS):
        def tile(i, carry):
            rows = span(i, 48)
            value = target[rows, :].astype(f32)
            for term in terms:
                value = value + term[rows, :].astype(f32)
            target[rows, :] = value.astype(bf16)
            return carry

        lax.fori_loop(0, count // 48, tile, 0)

    def core_slot(zz, yy):
        start = pl.multiple_of(lax.rem(yy, 2) * ROWS, 32)
        return core_in.at[zz * 2 + lax.div(yy, 2), pl.ds(start, ROWS), :]

    def gradient(j, far):
        zz = zs[j]
        g = zz * 2 + (kk if far else k)


        def tile(i, carry):
            rows = span(i, 384)
            w[g, rows, :] = matmul(hg[g, :, rows], delta[...], TN).astype(bf16)
            return carry

        lax.fori_loop(0, 2, tile, 0)
        for l in (3, 2) if far else (0, 1):
            scatter(j * 4 + l, chunk(zz, ys[l], oc), core_slot(zz, ys[l]), device(z, y, oc, x))

    def cores(j, l):
        scattered(j * 4 + l, core_slot(zs[j], ys[l]))
        add(chunk(zs[j], ys[l], c), [core_slot(zs[j], ys[l])])

    kinds = {0: y, 1: ya, 2: yp}
    down, up = device(zm, y, c, x), device(zp, y, c, x)

    def send_halves(kind):
        yy = kinds[kind]
        event = 16 + 4 * kind
        scatter(event, chunk(z2, yy, c, 0, ROWS // 2), zhalf_in.at[kind, 0], down)
        scatter(event + 1, chunk(z2, yy, c, ROWS // 2, ROWS // 2), zhalf_in.at[kind, 1], up)

    def send_full(kind, side):
        yy = kinds[kind]
        event = 16 + 4 * kind + side
        zz = (zm, zp)[side]
        scattered(event, zhalf_in.at[kind, side])
        add(
            chunk(zz, yy, c, side * (ROWS // 2), ROWS // 2),
            [zhalf_in.at[kind, side]],
            ROWS // 2,
        )
        scatter(event + 2, chunk(zz, yy, c), zfull_in.at[kind, side], (down, up)[side])

    def wait_fulls(kind):
        for side in range(2):
            scattered(18 + 4 * kind + side, zfull_in.at[kind, side])
        return [zfull_in.at[kind, side] for side in range(2)]

    def send_y(j):
        scatter(28 + j, chunk(zs[j], yap, c), y_in.at[j], device(z, ya, c, x))

    def take_y(j):
        scattered(28 + j, y_in.at[j])
        add(chunk(zs[j], yp, c), [y_in.at[j]])

    gradient(3, True)
    cores(3, 3)
    send_y(3)
    cores(3, 2)
    send_halves(1)
    gradient(3, False)
    cores(3, 0)
    send_halves(0)
    gradient(1, True)
    cores(1, 3)
    send_y(1)
    cores(3, 1)
    gradient(2, True)
    cores(2, 3)
    send_y(2)
    take_y(3)
    send_halves(2)
    cores(1, 2)
    send_full(1, 1)
    cores(2, 2)
    send_full(1, 0)
    gradient(0, True)
    cores(0, 3)
    send_y(0)
    gradient(1, False)
    cores(1, 0)
    send_full(0, 1)
    gradient(2, False)
    cores(2, 0)
    send_full(0, 0)
    cores(1, 1)
    take_y(1)
    send_full(2, 1)
    cores(2, 1)
    take_y(2)
    send_full(2, 0)
    gradient(0, False)
    cores(0, 2)
    add(chunk(z, ya, c), wait_fulls(1))
    scatter(32, chunk(z, ya, c), y_in.at[4], device(z, ya, c, x))
    cores(0, 1)
    cores(0, 0)
    take_y(0)
    add(chunk(z, yp, c), wait_fulls(2))
    scatter(33, chunk(z, yp, c), pair_in, device(z, yp, c, x))
    terms = wait_fulls(0)
    scattered(32, y_in.at[4])
    terms = terms + [y_in.at[4]]

    def finish(i, carry):
        rows = span(i, 48)
        value = own[rows, :].astype(f32)
        for term in terms:
            value = value + term[rows, :].astype(f32)
        grad_out[rows, span(half, COLS)] = value
        return carry

    lax.fori_loop(0, ROWS // 48, finish, 0)
    scattered(33, pair_in)
    grad_out[:, span(1 - half, COLS)] = pair_in[...].astype(f32)
    for copy in sends:
        copy.wait_send()


def step(row_count, patches, group, offset, gain, embed, readout, target, master):
    vmem = pl.BlockSpec(memory_space=pltpu.VMEM)
    smem = pl.BlockSpec(memory_space=pltpu.SMEM)
    hbm = pl.BlockSpec(memory_space=pl.ANY)
    dma = pltpu.SemaphoreType.DMA
    return pl.pallas_call(
        kernel,
        out_shape=(
            jax.ShapeDtypeStruct((640, 128), bf16),
            jax.ShapeDtypeStruct((ROWS, 2 * COLS), f32),
        ),
        in_specs=[smem, vmem, vmem, vmem, vmem, hbm, hbm, hbm, hbm],
        out_specs=(vmem, vmem),
        scratch_shapes=[
            pltpu.VMEM((128, WIDTH), bf16),
            pltpu.VMEM((COLS, 128), bf16),
            pltpu.VMEM((640, 128), bf16),
            pltpu.VMEM((ROWS, COLS), f32),
            pltpu.VMEM((ROWS, COLS), f32),
            pltpu.VMEM((ROWS, COLS), bf16),
            pltpu.VMEM((8, COLS, COLS), bf16),
            pltpu.VMEM((8, TOKENS, COLS), bf16),
            pltpu.VMEM((TOKENS, COLS), f32),
            pltpu.VMEM((TOKENS, COLS), bf16),
            pltpu.VMEM((TOKENS, 128), f32),
            pltpu.VMEM((8, 1, COLS), f32),
            pltpu.VMEM((512, 512), bf16),
            pltpu.VMEM((512, 256), bf16),
            pltpu.VMEM((512, 256), bf16),
            pltpu.VMEM((512, 256), bf16),
            pltpu.VMEM((SLOTS, 256), bf16),
            pltpu.VMEM((TOKENS, 128), bf16),
            pltpu.VMEM((8, BLOCK, 128), bf16),
            pltpu.VMEM((8, BLOCK, 128), bf16),
            pltpu.VMEM((BLOCK, 128), f32),
            pltpu.VMEM((BLOCK, 128), bf16),
            pltpu.VMEM((8, BLOCK, 128), bf16),
            pltpu.VMEM((8, 2 * ROWS, COLS), bf16),
            pltpu.VMEM((3, 2, ROWS // 2, COLS), bf16),
            pltpu.VMEM((3, 2, ROWS, COLS), bf16),
            pltpu.VMEM((5, ROWS, COLS), bf16),
            pltpu.VMEM((ROWS, COLS), bf16),
            dma((5,)),
            dma((16,)),
            dma((16,)),
            dma((8,)),
            dma((8,)),
            dma((8,)),
            dma((8,)),
            dma((34,)),
            dma((34,)),
            dma((8,)),
            dma((8,)),
            dma((8,)),
            dma((8,)),
            dma((34,)),
            dma((34,)),
        ],
        compiler_params=pltpu.CompilerParams(
            collective_id=0, has_side_effects=True, vmem_limit_bytes=56 * 1024 * 1024
        ),
        name="train_step",
    )(row_count, patches, group, offset, gain, embed, readout, target, master)


def shards(
    patches,
    row_count,
    target_group,
    target_offset,
    embed,
    norm_gain,
    readout,
    target,
    master,
    moment1,
    moment2,
):
    prediction, gradient = step(
        row_count,
        patches,
        target_group.reshape(3, 128),
        target_offset.reshape(3, 128),
        norm_gain.reshape(48, 128),
        embed,
        readout,
        target,
        master,
    )
    moment1_new = beta_one * moment1 + (1.0 - beta_one) * gradient
    moment2_new = beta_two * moment2 + (1.0 - beta_two) * gradient * gradient
    first_fix = moment1_new / (1.0 - beta_one**step_count)
    second_fix = moment2_new / (1.0 - beta_two**step_count)
    master_new = master - learn_rate * (
        first_fix / (jnp.sqrt(second_fix) + adam_epsilon) + decay_rate * master
    )
    return (
        prediction.astype(f32),
        master_new,
        moment1_new,
        moment2_new,
        master_new.astype(bf16),
    )


def solution(mesh):
    placed = (
        P(("dp", "mp"), None),
        P(("dp", "mp")),
        P(("dp", "mp")),
        P(("dp", "mp")),
        P(),
        P(),
        P("mp", None),
        P("dp", None),
        P("dp", "mp"),
        P("dp", "mp"),
        P("dp", "mp"),
    )
    return jax.shard_map(
        shards,
        mesh=mesh,
        in_specs=placed,
        out_specs=(P("dp", None), P("dp", "mp"), P("dp", "mp"), P("dp", "mp"), P("dp", "mp")),
        check_vma=False,
    )
```

```python
import jax
import jax.numpy as jnp
from jax import lax
from jax.experimental import pallas as pl
from jax.experimental.pallas import tpu as pltpu
from jax.sharding import PartitionSpec as P

gelu_const = 0.7978845608028654
cubic = 0.044715
beta_one = 0.9
beta_two = 0.95
learn_rate = 0.01
decay_rate = 0.1
adam_epsilon = 1e-08
step_count = 20

WIDTH = 6144
ROWS = 192
COLS = 768
TOKENS = 1280
BLOCK = 160
SLOTS = 384
SCALE = 1.0 / WIDTH**0.5
MESH = pl.DeviceIdType.MESH
f32, bf16, i32 = jnp.float32, jnp.bfloat16, jnp.int32

NN = (((1,), (0,)), ((), ()))
NT = (((1,), (1,)), ((), ()))
TN = (((0,), (0,)), ((), ()))


def matmul(a, b, dims=NN):
    return lax.dot_general(a, b, dims, preferred_element_type=f32)


def iota(shape, axis):
    return lax.broadcasted_iota(i32, shape, axis)


def kernel(
    row_count,
    patches,
    group_row,
    offset_row,
    gain,
    embed_hbm,
    readout_hbm,
    target_hbm,
    master_hbm,
    pred_out,
    grad_out,
    emb,
    ro,
    tgt,
    master_own,
    master_far,
    far_half,
    w,
    hg,
    acc,
    delta,
    ssq,
    gain_rows,
    perm,
    out1,
    in1,
    out2,
    in2,
    batch,
    part_out,
    part_in,
    part_own,
    err_own,
    err_in,
    core_in,
    zhalf_in,
    zfull_in,
    y_in,
    pair_in,
    local_sem,
    r1_send,
    r1_recv,
    r2_send,
    r2_recv,
    r3_send,
    r3_recv,
    ag_send,
    ag_recv,
    part_send,
    part_recv,
    err_send,
    err_recv,
    rs_send,
    rs_recv,
):
    dp, x = lax.axis_index("dp"), lax.axis_index("mp")
    z = lax.div(dp, 8)
    y = lax.rem(lax.div(dp, 2), 4)
    c = lax.rem(dp, 2)
    k = lax.div(y, 2)
    p = lax.rem(y, 2)
    half = lax.rem(p + k, 2)
    yp = y + 1 - 2 * p
    ya = 3 - y
    yap = 3 - yp
    kk, oc = 1 - k, 1 - c
    zp, zm, z2 = lax.rem(z + 1, 4), lax.rem(z + 3, 4), lax.rem(z + 2, 4)
    member = z * 4 + k * 2 + c
    sub = p * 4 + x
    zs = (z, zp, zm, z2)
    ys = (y, yp, ya, yap)

    def device(zz, yy, cc, xx):
        return ((zz * 4 + yy) * 2 + cc, xx)

    def member_device(i):
        other = lax.rem(member + i, 16)
        zz, kz, cc = lax.div(other, 4), lax.rem(lax.div(other, 2), 2), lax.rem(other, 2)
        return other, device(zz, 2 * kz + p, cc, x)

    def sub_device(i):
        other = lax.rem(sub + i, 8)
        return other, device(z, 2 * k + lax.div(other, 4), c, lax.rem(other, 4))

    def remote(src, dst, send, recv, to):
        return pltpu.make_async_remote_copy(
            src_ref=src, dst_ref=dst, send_sem=send, recv_sem=recv, device_id=to, device_id_type=MESH
        )

    def chunk(zz, yy, cc, low=0, count=ROWS):
        start = pl.multiple_of(lax.rem(yy, 2) * (2 * ROWS) + cc * ROWS + low, 32)
        return w.at[zz * 2 + lax.div(yy, 2), pl.ds(start, count), :]

    def span(index, size, count=None):
        return pl.ds(pl.multiple_of(index * size, size), size if count is None else count)

    barrier = pltpu.get_barrier_semaphore()
    peers = [member_device(i)[1] for i in range(1, 16)]
    peers += [sub_device(i)[1] for i in range(1, 8)]
    peers += [device(z, ya, c, x)]
    for peer in peers:
        pl.semaphore_signal(barrier, inc=1, device_id=peer, device_id_type=MESH)

    loads = [
        (master_hbm.at[:, span(half, COLS)], master_own),
        (master_hbm.at[:, span(1 - half, COLS)], master_far),
        (embed_hbm, emb),
        (readout_hbm.at[span(half, COLS), :], ro),
        (target_hbm, tgt),
    ]
    loads = [pltpu.make_async_copy(a, b, local_sem.at[i]) for i, (a, b) in enumerate(loads)]
    for load in loads:
        load.start()

    def as_row(ref):
        return jnp.concatenate([ref[i : i + 1, :] for i in range(SLOTS // 128)], axis=1)

    group, offset = as_row(group_row), as_row(offset_row)
    live = iota((1, SLOTS), 1) < row_count[0]
    to_member = (group >> 3) * 4 + ((group >> 2) & 1) * 2 + (group & 1)
    block = sum((offset >= BLOCK * i).astype(i32) for i in range(1, 4))
    place = offset - block * BLOCK + 1
    to_sub = ((group >> 1) & 1) * 4 + block
    key = jnp.where(live, to_member * 8 + to_sub, -1)
    row_id, col_id = iota((SLOTS, SLOTS), 0), iota((SLOTS, SLOTS), 1)

    def column(values):
        wide = jnp.broadcast_to(values.astype(f32), (SLOTS, SLOTS))
        return jnp.sum(jnp.where(row_id == col_id, wide, 0.0), axis=1, keepdims=True)

    same = (column(key) == key.astype(f32)) & (row_id < col_id)
    rank = jnp.sum(jnp.where(same, 1.0, 0.0), axis=0, keepdims=True).astype(i32)
    slot = jnp.where(live, to_member * 32 + rank * 8 + to_sub, -1)
    pick = jnp.where(iota((512, SLOTS), 0) == slot, 1.0, 0.0).astype(bf16)
    marks = jnp.broadcast_to(column(place), (SLOTS, 128)).astype(bf16)
    out1[:, :128] = matmul(pick, patches[...]).astype(bf16)
    out1[:, 128:] = matmul(pick, marks).astype(bf16)

    loads[0].wait()
    loads[1].wait()
    own = chunk(z, y, c)
    own[...] = master_own[...].astype(bf16)
    far_half[...] = master_far[...].astype(bf16)

    pl.semaphore_wait(barrier, len(peers))

    sends = []

    def launch(copy):
        copy.start()
        sends.append(copy)

    for i in range(1, 16):
        other, to = member_device(i)
        launch(
            remote(
                out1.at[span(other, 32), :],
                in1.at[span(member, 32), :],
                r1_send.at[other],
                r1_recv.at[member],
                to,
            )
        )

    def gather(event, src, dst, to):
        remote(src, dst, ag_send.at[event], ag_recv.at[event], to).start()

    def gathered(event, dst):
        remote(dst, dst, ag_send.at[event], ag_recv.at[event], device(z, y, oc, x)).wait_recv()

    def along_z(event, zz, yy, low=0, count=ROWS, up=True):
        piece = chunk(zz, yy, c, low, count)
        gather(event, piece, piece, device(zp if up else zm, y, c, x))

    def full_z(event, yy):
        along_z(event, z, yy)
        along_z(event + 1, z, yy, up=False)

    def halves_z(event, yy):
        along_z(event + 2, zm, yy, 0, ROWS // 2)
        along_z(event + 3, zp, yy, ROWS // 2, ROWS // 2, up=False)

    def wait_full(event, yy):
        gathered(event, chunk(zm, yy, c))
        gathered(event + 1, chunk(zp, yy, c))

    def wait_halves(event, yy):
        gathered(event + 2, chunk(z2, yy, c, 0, ROWS // 2))
        gathered(event + 3, chunk(z2, yy, c, ROWS // 2, ROWS // 2))

    def along_y(j):
        piece = chunk(zs[j], yp, c)
        gather(14 + j, piece, piece, device(z, ya, c, x))

    def wait_y(j):
        gathered(14 + j, chunk(zs[j], yap, c))

    def relay(j, l):
        piece = chunk(zs[j], ys[l], c)
        gather(18 + j * 4 + l, piece, piece, device(z, y, oc, x))

    def wait_relay(j, l):
        gathered(18 + j * 4 + l, chunk(zs[j], ys[l], oc))

    gather(0, far_half, own, device(z, yp, c, x))
    gather(1, own, own, device(z, ya, c, x))
    full_z(2, y)
    relay(0, 0)

    gains = gain[...].astype(f32)
    lanes = COLS // 128
    for j in range(8):
        rows = [gains[lanes * j + l : lanes * j + l + 1] for l in range(lanes)]
        gain_rows[j] = jnp.concatenate(rows, axis=1)
    ssq[...] = jnp.zeros_like(ssq)
    acc[...] = jnp.zeros_like(acc)
    in1[span(member, 32), :] = out1[span(member, 32), :]
    row512 = iota((512, 512), 0)
    source = (row512 & 15) * 32 + ((row512 >> 4) & 3) * 8 + (row512 >> 6)
    perm[...] = jnp.where(iota((512, 512), 1) == source, 1.0, 0.0).astype(bf16)
    for i in range(1, 16):
        other, to = member_device(i)
        landed = in1.at[span(other, 32), :]
        remote(landed, landed, r1_send.at[other], r1_recv.at[other], to).wait_recv()
    out2[...] = matmul(perm[...], in1[...]).astype(bf16)
    for i in range(1, 8):
        other, to = sub_device(i)
        launch(
            remote(
                out2.at[span(other, 64, 48), :],
                in2.at[span(sub, 48), :],
                r2_send.at[other],
                r2_recv.at[sub],
                to,
            )
        )
    in2[span(sub, 48), :] = out2[span(sub, 64, 48), :]

    gathered(0, chunk(z, yp, c))
    full_z(10, yp)
    along_y(0)
    relay(0, 1)

    for i in range(1, 8):
        other, to = sub_device(i)
        landed = in2.at[span(other, 48), :]
        remote(landed, landed, r2_send.at[other], r2_recv.at[other], to).wait_recv()
    mark = in2[:, 128:].astype(f32)
    lane = iota((SLOTS, 128), 1)
    to_place = jnp.concatenate(
        [
            jnp.where(mark == (lane + 1).astype(f32), 1.0, 0.0),
            jnp.where(mark == (lane + 129).astype(f32), 1.0, 0.0),
        ],
        axis=1,
    ).astype(bf16)
    mine = span(sub, BLOCK)
    batch[mine, :] = matmul(to_place, in2[:, :128], TN)[:BLOCK].astype(bf16)
    for i in range(1, 8):
        other, to = sub_device(i)
        launch(remote(batch.at[mine, :], batch.at[mine, :], r3_send.at[other], r3_recv.at[sub], to))

    wait_full(2, y)
    relay(1, 0)
    relay(2, 0)
    gathered(1, chunk(z, ya, c))
    relay(0, 2)
    wait_full(10, yp)
    along_y(1)
    along_y(2)
    halves_z(10, yp)
    full_z(6, ya)
    relay(1, 1)
    relay(2, 1)

    for i in range(1, 8):
        other, to = sub_device(i)
        landed = batch.at[span(other, BLOCK), :]
        remote(landed, landed, r3_send.at[other], r3_recv.at[other], to).wait_recv()
    loads[2].wait()

    def embed(j, carry):
        @pl.when(j == 3)
        def _():
            wait_halves(10, yp)
            halves_z(2, y)
            relay(3, 1)
            wait_y(0)
            relay(0, 3)

        @pl.when(j == 5)
        def _():
            along_y(3)
            wait_full(6, ya)
            halves_z(6, ya)
            relay(1, 2)
            relay(2, 2)

        v = matmul(batch[...], emb[:, span(j, COLS)])
        t = jnp.tanh(v * (gelu_const + (gelu_const * cubic) * (v * v)))
        twice = v + v * t
        square = twice * twice
        total = sum(square[:, l * 128 : (l + 1) * 128] for l in range(COLS // 128))
        ssq[...] += total
        hg[j] = (twice * gain_rows[j]).astype(bf16)
        return carry

    lax.fori_loop(0, 8, embed, 0)

    def forward(i, carry):
        @pl.when(i == 0)
        def _():
            for l in range(2):
                wait_relay(0, l)

        @pl.when(i == 1)
        def _():
            for l in range(2, 4):
                wait_relay(0, l)

        @pl.when(i == 2)
        def _():
            for l in range(2):
                wait_relay(1, l)

        @pl.when(i == 3)
        def _():
            wait_y(1)
            relay(1, 3)
            wait_halves(2, y)
            relay(3, 0)
            for l in range(2, 4):
                wait_relay(1, l)

        @pl.when(i == 4)
        def _():
            wait_y(2)
            relay(2, 3)
            for l in range(2):
                wait_relay(2, l)

        @pl.when(i == 5)
        def _():
            wait_halves(6, ya)
            relay(3, 2)
            for l in range(2, 4):
                wait_relay(2, l)

        @pl.when(i == 6)
        def _():
            for l in range(2):
                wait_relay(3, l)

        @pl.when(i == 7)
        def _():
            wait_y(3)
            relay(3, 3)
            for l in range(2, 4):
                wait_relay(3, l)

        j, far = lax.div(i, 2), lax.rem(i, 2)
        zz = lax.rem(z + j + lax.div(j, 2) - 2 * lax.div(j, 3), 4)
        g = zz * 2 + k + far * (1 - 2 * k)
        acc[...] += matmul(hg[g], w[g])
        return carry

    lax.fori_loop(0, 8, forward, 0)

    loads[3].wait()
    loads[4].wait()

    def row_scale(rows):
        mean4 = jnp.sum(ssq[rows, :], axis=1, keepdims=True) * (0.25 / WIDTH)
        return lax.rsqrt(mean4 + 1e-05) * (0.5 * SCALE)

    def partial(index):
        rows = span(index, BLOCK)
        v = acc[rows, :] * row_scale(rows)
        t = jnp.tanh(v * (gelu_const + (gelu_const * cubic) * (v * v)))
        return matmul((0.5 * v * (1.0 + t)).astype(bf16), ro[...])

    for i in range(1, 8):
        other, to = sub_device(i)
        part_out[other] = partial(other).astype(bf16)
        launch(
            remote(part_out.at[other], part_in.at[sub], part_send.at[other], part_recv.at[sub], to)
        )
    part_own[...] = partial(sub)

    def slope(i, carry):
        rows = span(i, BLOCK)
        r = row_scale(rows)
        v = acc[rows, :] * r
        t = jnp.tanh(v * (gelu_const + (gelu_const * cubic) * (v * v)))
        acc[rows, :] = r * (
            0.5 * (1.0 + t)
            + (0.5 * gelu_const) * v * (1.0 - t * t) * (1.0 + (3.0 * cubic) * (v * v))
        )
        return carry

    lax.fori_loop(0, 8, slope, 0)
    total = part_own[...]
    for i in range(1, 8):
        other, to = sub_device(i)
        landed = part_in.at[other]
        remote(landed, landed, part_send.at[other], part_recv.at[other], to).wait_recv()
        total = total + part_in[other].astype(f32)
    total = total.astype(bf16)
    err_in[sub] = total
    err_own[...] = (total.astype(f32) - tgt[span(x, BLOCK), :].astype(f32)).astype(bf16)
    for i in range(4):
        other = lax.rem(x + i, 4)
        launch(
            remote(
                err_own,
                err_in.at[sub],
                err_send.at[(1 - p) * 4 + other],
                err_recv.at[sub],
                device(z, yp, c, other),
            )
        )
        if i:
            launch(
                remote(
                    err_in.at[sub],
                    err_in.at[sub],
                    err_send.at[p * 4 + other],
                    err_recv.at[sub],
                    device(z, y, c, other),
                )
            )

    def backward(index, errors):
        rows = span(index, BLOCK)
        delta[rows, :] = (matmul(errors, ro[...], NT) * acc[rows, :]).astype(bf16)

    for i in range(4):
        other = lax.rem(x + i, 4)
        index = p * 4 + other
        landed = err_in.at[index]
        if i:
            to = device(z, y, c, other)
            remote(landed, landed, err_send.at[index], err_recv.at[index], to).wait_recv()
        rows = span(other, BLOCK)
        pred_out[rows, :] = err_in[index]
        backward(index, (err_in[index].astype(f32) - tgt[rows, :].astype(f32)).astype(bf16))
    for i in range(4):
        other = lax.rem(x + i, 4)
        index = (1 - p) * 4 + other
        landed = err_in.at[index]
        to = device(z, yp, c, other)
        remote(landed, landed, err_send.at[index], err_recv.at[index], to).wait_recv()
        backward(index, err_in[index])

    for event in range(34):
        piece = far_half.at[: ROWS // 2, :] if event in (4, 5, 8, 9, 12, 13) else far_half
        to = device(z, y, oc, x)
        remote(piece, piece, ag_send.at[event], ag_recv.at[event], to).wait_send()

    def scatter(event, src, dst, to):
        launch(remote(src, dst, rs_send.at[event], rs_recv.at[event], to))

    def scattered(event, dst):
        remote(dst, dst, rs_send.at[event], rs_recv.at[event], device(z, y, oc, x)).wait_recv()

    def add(target, terms, count=ROWS):
        def tile(i, carry):
            rows = span(i, 48)
            value = target[rows, :].astype(f32)
            for term in terms:
                value = value + term[rows, :].astype(f32)
            target[rows, :] = value.astype(bf16)
            return carry

        lax.fori_loop(0, count // 48, tile, 0)

    def core_slot(zz, yy):
        start = pl.multiple_of(lax.rem(yy, 2) * ROWS, 32)
        return core_in.at[zz * 2 + lax.div(yy, 2), pl.ds(start, ROWS), :]

    def gradient(j, far):
        zz = zs[j]
        g = zz * 2 + (kk if far else k)


        def tile(i, carry):
            rows = span(i, 384)
            w[g, rows, :] = matmul(hg[g, :, rows], delta[...], TN).astype(bf16)
            return carry

        lax.fori_loop(0, 2, tile, 0)
        for l in (3, 2) if far else (0, 1):
            scatter(j * 4 + l, chunk(zz, ys[l], oc), core_slot(zz, ys[l]), device(z, y, oc, x))

    def cores(j, l):
        scattered(j * 4 + l, core_slot(zs[j], ys[l]))
        add(chunk(zs[j], ys[l], c), [core_slot(zs[j], ys[l])])

    kinds = {0: y, 1: ya, 2: yp}
    down, up = device(zm, y, c, x), device(zp, y, c, x)

    def send_halves(kind):
        yy = kinds[kind]
        event = 16 + 4 * kind
        scatter(event, chunk(z2, yy, c, 0, ROWS // 2), zhalf_in.at[kind, 0], down)
        scatter(event + 1, chunk(z2, yy, c, ROWS // 2, ROWS // 2), zhalf_in.at[kind, 1], up)

    def send_full(kind, side):
        yy = kinds[kind]
        event = 16 + 4 * kind + side
        zz = (zm, zp)[side]
        scattered(event, zhalf_in.at[kind, side])
        add(
            chunk(zz, yy, c, side * (ROWS // 2), ROWS // 2),
            [zhalf_in.at[kind, side]],
            ROWS // 2,
        )
        scatter(event + 2, chunk(zz, yy, c), zfull_in.at[kind, side], (down, up)[side])

    def wait_fulls(kind):
        for side in range(2):
            scattered(18 + 4 * kind + side, zfull_in.at[kind, side])
        return [zfull_in.at[kind, side] for side in range(2)]

    def send_y(j):
        scatter(28 + j, chunk(zs[j], yap, c), y_in.at[j], device(z, ya, c, x))

    def take_y(j):
        scattered(28 + j, y_in.at[j])
        add(chunk(zs[j], yp, c), [y_in.at[j]])

    gradient(3, True)
    cores(3, 3)
    send_y(3)
    cores(3, 2)
    send_halves(1)
    gradient(3, False)
    cores(3, 0)
    send_halves(0)
    gradient(1, True)
    cores(1, 3)
    send_y(1)
    cores(3, 1)
    gradient(2, True)
    cores(2, 3)
    send_y(2)
    take_y(3)
    send_halves(2)
    cores(1, 2)
    send_full(1, 1)
    cores(2, 2)
    send_full(1, 0)
    gradient(1, False)
    cores(1, 0)
    send_full(0, 1)
    gradient(2, False)
    cores(2, 0)
    send_full(0, 0)
    gradient(0, True)
    cores(0, 3)
    send_y(0)
    gradient(0, False)
    cores(1, 1)
    cores(2, 1)
    cores(0, 2)
    take_y(1)
    send_full(2, 1)
    take_y(2)
    send_full(2, 0)
    add(chunk(z, ya, c), wait_fulls(1))
    scatter(32, chunk(z, ya, c), y_in.at[4], device(z, ya, c, x))
    cores(0, 1)
    cores(0, 0)
    take_y(0)
    add(chunk(z, yp, c), wait_fulls(2))
    scatter(33, chunk(z, yp, c), pair_in, device(z, yp, c, x))
    terms = wait_fulls(0)
    scattered(32, y_in.at[4])
    terms = terms + [y_in.at[4]]

    def finish(i, carry):
        rows = span(i, 48)
        value = own[rows, :].astype(f32)
        for term in terms:
            value = value + term[rows, :].astype(f32)
        grad_out[rows, span(half, COLS)] = value
        return carry

    lax.fori_loop(0, ROWS // 48, finish, 0)
    scattered(33, pair_in)
    grad_out[:, span(1 - half, COLS)] = pair_in[...].astype(f32)
    for copy in sends:
        copy.wait_send()


def step(row_count, patches, group, offset, gain, embed, readout, target, master):
    vmem = pl.BlockSpec(memory_space=pltpu.VMEM)
    smem = pl.BlockSpec(memory_space=pltpu.SMEM)
    hbm = pl.BlockSpec(memory_space=pl.ANY)
    dma = pltpu.SemaphoreType.DMA
    return pl.pallas_call(
        kernel,
        out_shape=(
            jax.ShapeDtypeStruct((640, 128), bf16),
            jax.ShapeDtypeStruct((ROWS, 2 * COLS), f32),
        ),
        in_specs=[smem, vmem, vmem, vmem, vmem, hbm, hbm, hbm, hbm],
        out_specs=(vmem, vmem),
        scratch_shapes=[
            pltpu.VMEM((128, WIDTH), bf16),
            pltpu.VMEM((COLS, 128), bf16),
            pltpu.VMEM((640, 128), bf16),
            pltpu.VMEM((ROWS, COLS), f32),
            pltpu.VMEM((ROWS, COLS), f32),
            pltpu.VMEM((ROWS, COLS), bf16),
            pltpu.VMEM((8, COLS, COLS), bf16),
            pltpu.VMEM((8, TOKENS, COLS), bf16),
            pltpu.VMEM((TOKENS, COLS), f32),
            pltpu.VMEM((TOKENS, COLS), bf16),
            pltpu.VMEM((TOKENS, 128), f32),
            pltpu.VMEM((8, 1, COLS), f32),
            pltpu.VMEM((512, 512), bf16),
            pltpu.VMEM((512, 256), bf16),
            pltpu.VMEM((512, 256), bf16),
            pltpu.VMEM((512, 256), bf16),
            pltpu.VMEM((SLOTS, 256), bf16),
            pltpu.VMEM((TOKENS, 128), bf16),
            pltpu.VMEM((8, BLOCK, 128), bf16),
            pltpu.VMEM((8, BLOCK, 128), bf16),
            pltpu.VMEM((BLOCK, 128), f32),
            pltpu.VMEM((BLOCK, 128), bf16),
            pltpu.VMEM((8, BLOCK, 128), bf16),
            pltpu.VMEM((8, 2 * ROWS, COLS), bf16),
            pltpu.VMEM((3, 2, ROWS // 2, COLS), bf16),
            pltpu.VMEM((3, 2, ROWS, COLS), bf16),
            pltpu.VMEM((5, ROWS, COLS), bf16),
            pltpu.VMEM((ROWS, COLS), bf16),
            dma((5,)),
            dma((16,)),
            dma((16,)),
            dma((8,)),
            dma((8,)),
            dma((8,)),
            dma((8,)),
            dma((34,)),
            dma((34,)),
            dma((8,)),
            dma((8,)),
            dma((8,)),
            dma((8,)),
            dma((34,)),
            dma((34,)),
        ],
        compiler_params=pltpu.CompilerParams(
            collective_id=0, has_side_effects=True, vmem_limit_bytes=56 * 1024 * 1024
        ),
        name="train_step",
    )(row_count, patches, group, offset, gain, embed, readout, target, master)


def shards(
    patches,
    row_count,
    target_group,
    target_offset,
    embed,
    norm_gain,
    readout,
    target,
    master,
    moment1,
    moment2,
):
    prediction, gradient = step(
        row_count,
        patches,
        target_group.reshape(3, 128),
        target_offset.reshape(3, 128),
        norm_gain.reshape(48, 128),
        embed,
        readout,
        target,
        master,
    )
    moment1_new = beta_one * moment1 + (1.0 - beta_one) * gradient
    moment2_new = beta_two * moment2 + (1.0 - beta_two) * gradient * gradient
    first_fix = moment1_new / (1.0 - beta_one**step_count)
    second_fix = moment2_new / (1.0 - beta_two**step_count)
    master_new = master - learn_rate * (
        first_fix / (jnp.sqrt(second_fix) + adam_epsilon) + decay_rate * master
    )
    return (
        prediction.astype(f32),
        master_new,
        moment1_new,
        moment2_new,
        master_new.astype(bf16),
    )


def solution(mesh):
    placed = (
        P(("dp", "mp"), None),
        P(("dp", "mp")),
        P(("dp", "mp")),
        P(("dp", "mp")),
        P(),
        P(),
        P("mp", None),
        P("dp", None),
        P("dp", "mp"),
        P("dp", "mp"),
        P("dp", "mp"),
    )
    return jax.shard_map(
        shards,
        mesh=mesh,
        in_specs=placed,
        out_specs=(P("dp", None), P("dp", "mp"), P("dp", "mp"), P("dp", "mp"), P("dp", "mp")),
        check_vma=False,
    )
```
